128 devices in a mesh: hi: 8 (over x_hi, z), lo: 16 (over y, x_lo, core).
Axes of the slice: x: 4 (x_hi: 2, x_lo: 2; x = x_hi * 2 + x_lo), y: 4, z: 4, core: 2. Of those that a mesh axis runs over, the one named last changes fastest.
Arguments:
- amplitudes: float32 [2, 128, 262144], P(None, ('hi', 'lo')), may hold values from -20 to 20
- gate_picks: int32 [2, 25], replicated, may hold values from 0 to 2
- pair_qubits: int32 [2, 10, 2], replicated, may hold values from 0 to 24, as said below
- angles: float32 [2, 10], replicated, may hold values from -3.140625 to 3.140625
Outputs:
- final_state: float32 [2, 128, 262144], P(None, ('hi', 'lo'))
- marginal: float32 [128], replicated
The draws below stay inside these ranges and needn't reach their ends.
Inputs may be any that keep to these rules, and one draw needn't show every extreme that they name: `pair_qubits`: in each layer the 20 qubits named are all different; qubit 0 and qubit 25 - 1 are named in every layer.
All inputs are finite; a program needn't handle non-finite values.
Results may differ from the reference program's by a relative error of at most 0.0001.
Values sent between devices are 32-bit elements; how exact they have to be, the bound alone decides.
A program may use at most 128 MiB of HBM per device.

```python
import jax
import jax.numpy as jnp
from jax import lax

LAYERS = 2
PAIRS = 10
BLOCKS = 128
LOCAL = 262144
QUBITS = 25


def draw_amplitudes(key, part):
    key = jax.random.fold_in(key, 11)
    normal_key = jax.random.fold_in(key, 1)
    scale_key = jax.random.fold_in(key, 2)
    full_shape = (2, BLOCKS, LOCAL)
    trend_scale = 3.0 ** (lax.broadcasted_iota(jnp.float32, full_shape, 1) / max(BLOCKS - 1, 1) - 0.5)
    rough_scale = 10.0 ** (jax.random.uniform(scale_key, full_shape, jnp.float32) - 0.5)
    noise_part = jnp.clip(jax.random.normal(normal_key, full_shape, jnp.float32), -6.0, 6.0)
    return (noise_part * rough_scale * trend_scale * 0.5).astype(jnp.float32)


def draw_pair_qubits(key, part):
    key = jax.random.fold_in(key, 23)
    layer_list = []
    for layer_step in range(LAYERS):
        layer_key = jax.random.fold_in(key, layer_step)
        inner_part = jax.random.permutation(jax.random.fold_in(layer_key, 1), QUBITS - 2)[:2 * PAIRS - 2] + 1
        chosen = jnp.concatenate([jnp.array([0, QUBITS - 1], jnp.int32), inner_part.astype(jnp.int32)])
        ordering = jax.random.permutation(jax.random.fold_in(layer_key, 2), 2 * PAIRS)
        layer_list.append(chosen[ordering].reshape(PAIRS, 2))
    return jnp.stack(layer_list).astype(jnp.int32)


def touch_ends(entries, stream_key, smallest, top_value):
    index_at = [jax.random.randint(jax.random.fold_in(stream_key, axis), (), 0, length) for axis, length in enumerate(entries.shape)]
    main_axis = entries.shape.index(max(entries.shape))
    beside = index_at[:main_axis] + [(index_at[main_axis] + 1) % entries.shape[main_axis]] + index_at[main_axis + 1:]
    return entries.at[tuple(index_at)].set(smallest).at[tuple(beside)].set(top_value)


def setup_inputs(seed: int = 0) -> dict:
    streams_of = jax.random.split(jax.random.key(seed), 5)
    amplitudes = draw_amplitudes(jax.random.fold_in(streams_of[4], 71), 0)
    gate_picks = touch_ends(jax.random.randint(streams_of[1], (LAYERS, QUBITS), 0, 3), jax.random.fold_in(streams_of[1], 1), 0, 2).astype(jnp.int32)
    pair_qubits = draw_pair_qubits(jax.random.fold_in(streams_of[4], 71), 0)
    angles = jnp.clip(jax.random.uniform(streams_of[3], (LAYERS, PAIRS), jnp.float32, -3.140625, 3.140625), -3.140625, 3.140625)
    return dict(amplitudes=amplitudes, gate_picks=gate_picks, pair_qubits=pair_qubits, angles=angles)


one_half = 0.5
root_half = 0.7071067811865476
gate_real = [[[one_half, one_half], [one_half, one_half]], [[one_half, -one_half], [one_half, one_half]], [[root_half, -one_half], [one_half, root_half]]]
gate_imag = [[[one_half, -one_half], [-one_half, one_half]], [[one_half, -one_half], [one_half, one_half]], [[0.0, -one_half], [-one_half, 0.0]]]


def pick_gate(selector):
    chooser = (selector == jnp.arange(3, dtype=jnp.int32)).astype(jnp.float32)
    table_r = jnp.array(gate_real, jnp.float32)
    table_i = jnp.array(gate_imag, jnp.float32)
    return jnp.sum(chooser[:, None, None] * table_r, axis=0), jnp.sum(chooser[:, None, None] * table_i, axis=0)


def apply_qubit(real_part, imag_part, gate_r, gate_i, position, count):
    full_shape = (count >> (position + 1), 2, 1 << position)
    rows_r = real_part.reshape(full_shape)
    rows_i = imag_part.reshape(full_shape)
    r_zero, r_one = rows_r[:, 0], rows_r[:, 1]
    i_zero, i_one = rows_i[:, 0], rows_i[:, 1]
    out_r = []
    out_i = []
    for row_no in range(2):
        out_r.append(gate_r[row_no, 0] * r_zero - gate_i[row_no, 0] * i_zero + gate_r[row_no, 1] * r_one - gate_i[row_no, 1] * i_one)
        out_i.append(gate_r[row_no, 0] * i_zero + gate_i[row_no, 0] * r_zero + gate_r[row_no, 1] * i_one + gate_i[row_no, 1] * r_one)
    return jnp.stack(out_r, 1).reshape(-1), jnp.stack(out_i, 1).reshape(-1)


def reference(amplitudes, gate_picks, pair_qubits, angles):
    count = BLOCKS * LOCAL
    real_part = amplitudes[0].reshape(-1)
    imag_part = amplitudes[1].reshape(-1)
    flat_index = lax.iota(jnp.int32, count)
    for layer_step in range(LAYERS):
        for position in range(QUBITS):
            gate_r, gate_i = pick_gate(gate_picks[layer_step, position])
            real_part, imag_part = apply_qubit(real_part, imag_part, gate_r, gate_i, position, count)
        phase_sum = jnp.zeros((count,), jnp.float32)
        for pair_no in range(PAIRS):
            both_set = (jnp.right_shift(flat_index, pair_qubits[layer_step, pair_no, 0]) & jnp.right_shift(flat_index, pair_qubits[layer_step, pair_no, 1]) & 1).astype(jnp.float32)
            phase_sum = phase_sum + angles[layer_step, pair_no] * both_set
        cosine = jnp.cos(phase_sum)
        sine_part = jnp.sin(phase_sum)
        real_part, imag_part = real_part * cosine - imag_part * sine_part, real_part * sine_part + imag_part * cosine
    final_state = jnp.stack([real_part, imag_part]).reshape(2, BLOCKS, LOCAL)
    squared = (real_part * real_part + imag_part * imag_part).reshape(BLOCKS, BLOCKS, LOCAL // BLOCKS)
    marginal = jnp.sum(squared, axis=(0, 2)) / LOCAL
    return final_state, marginal
```

```python
import functools
import math

import jax
import jax.numpy as jnp
from jax import lax
from jax.experimental import pallas as pl
from jax.experimental.pallas import tpu as pltpu
from jax.sharding import PartitionSpec as P

MESH = pl.DeviceIdType.MESH

PHASE_IN = (-2, 4, 5)
PHASE_OUT = (-2, 0, -1)
PHASE_ALL = (1, 1, 0)

ROW_BITS = (0, 4, 5, 2, 3, 1, 6)
CHUNK_QUBITS = (9, 10)
CHUNKS = 4
SIZE = {"x": 4, "y": 4, "z": 4, "c": 2}
DIM = {"x": 0, "y": 1, "z": 2, "c": 3}

ORDER = ("xczy", "yxcz", "zyxc", "czyx")


def coordinates():
    hi, lo = lax.axis_index("hi"), lax.axis_index("lo")
    return {
        "x": (hi // 4) * 2 + (lo // 2) % 2,
        "y": lo // 4,
        "z": hi % 4,
        "c": lo % 2,
    }


def device_at(pos):
    return ((pos["x"] // 2) * 4 + pos["z"], pos["y"] * 4 + (pos["x"] % 2) * 2 + pos["c"])


def moved(pos, **flips):
    return device_at({a: jnp.bitwise_xor(pos[a], flips[a]) if flips.get(a, 0) else pos[a] for a in pos})


def hadamard(tiles):
    tiles = list(tiles)
    step = 1
    while step < len(tiles):
        for i in range(len(tiles)):
            if not i & step:
                a, b = tiles[i], tiles[i + step]
                tiles[i], tiles[i + step] = a + b, a - b
        step *= 2
    return tiles


def choose(table, pick):
    return jnp.where(pick == 0, table[0], jnp.where(pick == 1, table[1], table[2]))


def parity_sign(value):
    value = value ^ (value >> 4)
    value = value ^ (value >> 2)
    value = value ^ (value >> 1)
    return 1.0 - 2.0 * (value & 1).astype(jnp.float32)


def split(value):
    high = value.astype(jnp.bfloat16)
    low = (value - high.astype(jnp.float32)).astype(jnp.bfloat16)
    return jnp.concatenate([high, low], axis=1)


def part(ref, slot, at):
    index = [slot] + [at.get(a, slice(None)) for a in "xyzc"]
    return ref.at[tuple(index)]


def kernel(
    x_hbm,
    picks,
    pairs,
    angles,
    out_hbm,
    marginal_ref,
    st,
    vin,
    vout,
    tab_c,
    tab_s,
    in_c,
    in_s,
    fac_c,
    fac_s,
    work,
    acc,
    lanes_mat,
    rows_mat,
    mass_a,
    mass_b,
    in_sem,
    out_sem,
    send_sem,
    recv_sem,
    last_sem,
    mass_send,
    mass_recv,
):
    pos = coordinates()
    me = lax.axis_index("hi") * 16 + lax.axis_index("lo")

    def load(b):
        rows = pl.ds(b * 16, 16)
        return pltpu.make_async_copy(x_hbm.at[:, rows], vin.at[:, rows], in_sem.at[b])

    for b in range(8):
        load(b).start()

    barrier = pltpu.get_barrier_semaphore()
    flips = [{"z": z, "c": c} for z in range(4) for c in range(2) if z or c]
    flips += [{"x": x, "y": y} for x in range(4) for y in range(4) if x or y]
    for flip in flips:
        pl.semaphore_signal(barrier, inc=1, device_id=moved(pos, **flip), device_id_type=MESH)

    lane = lax.broadcasted_iota(jnp.int32, (8, 128), 1)
    sub = lax.broadcasted_iota(jnp.int32, (8, 128), 0)
    top = sub < 4
    side = jnp.where(top, -1.0, 1.0)
    local_n = lane | ((sub & 3) << 7)
    eighth = math.pi / 4

    lin_in = [choose(PHASE_IN, picks[0, q]) for q in range(25)]
    n_first = local_n | (me << 18)
    turn = jnp.zeros((8, 128), jnp.int32)
    for q in list(range(9)) + list(range(18, 25)):
        turn = turn + ((n_first >> q) & 1) * lin_in[q]
    for k in range(8):
        angle = ((turn + k) & 7).astype(jnp.float32) * eighth
        in_c[k] = jnp.cos(angle)
        in_s[k] = jnp.sin(angle) * side

    def swap(value):
        return pltpu.roll(value, 4, 0)

    def first_rows(i, _):
        xh, z, y = i // 16, (i // 4) % 4, i % 4
        k0 = xh * lin_in[17] + (z // 2) * lin_in[16] + (z % 2) * lin_in[15] + (y // 2) * lin_in[14] + (y % 2) * lin_in[13]
        for xl in range(2):
            for c in range(2):
                m = i * 4 + xl * 2 + c
                k1 = k0 + xl * lin_in[12] + c * lin_in[11]
                tiles = []
                for t in range(2):
                    re = vin[0, m, pl.ds(8 * t, 8)]
                    im = vin[1, m, pl.ds(8 * t, 8)]
                    rre, rim = swap(re), swap(im)
                    for e in range(2):
                        k = (k1 + t * lin_in[10] + e * lin_in[9]) & 7
                        if e == 0:
                            p, pr = jnp.where(top, re, rim), jnp.where(top, im, rre)
                        else:
                            p, pr = jnp.where(top, rre, im), jnp.where(top, rim, re)
                        tiles.append(p * in_c[k] + pr * in_s[k])
                tiles = hadamard(tiles)
                for j in range(CHUNKS):
                    st[j, 2 * xh + xl, y, z, c] = tiles[j]
        return 0

    for b in range(8):
        load(b).wait()
        lax.fori_loop(b * 4, b * 4 + 4, first_rows, 0)

    def walsh_rows(slot, mass=None):
        def pass_xy(i, _):
            z, c = i // 2, i % 2
            tiles = hadamard([st[slot, x, y, z, c] for x in range(4) for y in range(4)])
            for x in range(4):
                for y in range(4):
                    st[slot, x, y, z, c] = tiles[x * 4 + y]
            return 0

        def pass_zc(i, _):
            x, y = i // 4, i % 4
            tiles = hadamard([st[slot, x, y, z, c] for z in range(4) for c in range(2)])
            for z in range(4):
                for c in range(2):
                    tile = tiles[z * 2 + c]
                    st[slot, x, y, z, c] = tile
                    if mass == 0:
                        acc[x, y, z, c] = tile * tile
                    elif mass is not None:
                        acc[x, y, z, c] = acc[x, y, z, c] + tile * tile
            return 0

        lax.fori_loop(0, 8, pass_xy, 0)
        lax.fori_loop(0, 16, pass_zc, 0)

    def slot_of(e, i, j):
        return e * 20 + i * 4 + j

    def half(j, h):
        d = ORDER[j][3]
        width = SIZE[d] // 2
        return d, pl.ds(jnp.bitwise_xor(pos[d] // width, h) * width, width)

    def send_step(e, j, i, h):
        a = ORDER[j][i]
        if i < 3:
            d, piece = half(j, h)
            for flip in range(SIZE[a]):
                target = jnp.bitwise_xor(pos[a], flip) if flip else pos[a]
                src = part(st, slot_of(e, i, j), {a: target, d: piece})
                dst = part(st, slot_of(e, i + 1, j), {a: pos[a], d: piece})
                if flip:
                    pltpu.make_async_remote_copy(
                        src,
                        dst,
                        send_sem.at[e, j, i],
                        recv_sem.at[e, j, i, h],
                        device_id=moved(pos, **{a: flip}),
                        device_id_type=MESH,
                    ).start()
                else:
                    pltpu.make_async_copy(src, dst, recv_sem.at[e, j, i, h]).start()
        else:
            width = SIZE[a] // 2
            for flip in range(h * width, h * width + width):
                target = jnp.bitwise_xor(pos[a], flip) if flip else pos[a]
                src = part(st, slot_of(e, i, j), {a: target})
                dst = part(st, slot_of(e, i + 1, j), {a: pos[a]})
                if flip:
                    pltpu.make_async_remote_copy(
                        src,
                        dst,
                        send_sem.at[e, j, i],
                        last_sem.at[e, j],
                        device_id=moved(pos, **{a: flip}),
                        device_id_type=MESH,
                    ).start()
                else:
                    pltpu.make_async_copy(src, dst, last_sem.at[e, j]).start()

    def arrived_step(e, j, i, h):
        if i < 3:
            d, piece = half(j, h)
            ref = part(st, slot_of(e, i + 1, j), {d: piece})
            pltpu.make_async_copy(ref, ref, recv_sem.at[e, j, i, h]).wait()
        else:
            ref = st.at[slot_of(e, 4, j)]
            pltpu.make_async_copy(ref, ref, last_sem.at[e, j]).wait()

    def sent(e, steps):
        for j in range(CHUNKS):
            for i in steps:
                a = ORDER[j][i]
                ref = part(st, slot_of(e, i, j), {a: pl.ds(0, SIZE[a] * 3 // 4 if SIZE[a] == 4 else 1)})
                pltpu.make_async_copy(ref, ref, send_sem.at[e, j, i]).wait()

    def travel(e):
        for i in range(1, 4):
            for h in (1, 0):
                for j in range(CHUNKS):
                    arrived_step(e, j, i - 1, h)
                    send_step(e, j, i, h)

    pl.semaphore_wait(barrier, len(flips))
    for j in range(CHUNKS):
        walsh_rows(j)
        for h in (1, 0):
            send_step(0, j, 0, h)

    def phase_table(layer, n_base, row_base, linear, constant, scale):
        tile_qubits = [row_base + b for b in ROW_BITS] + list(CHUNK_QUBITS)
        other = [q for q in range(25) if q not in tile_qubits]
        first = [pairs[layer, k, 0] for k in range(10)]
        second = [pairs[layer, k, 1] for k in range(10)]
        theta = [angles[layer, k] for k in range(10)]
        n0 = local_n | n_base
        turns = jnp.full((8, 128), 0, jnp.int32) + constant
        for q in other:
            turns = turns + ((n0 >> q) & 1) * linear[q]
        phase = jnp.zeros((8, 128), jnp.float32)
        for k in range(10):
            both = (n0 >> first[k]) & (n0 >> second[k]) & 1
            phase = phase + theta[k] * both.astype(jnp.float32)
        phase = phase + (turns & 7).astype(jnp.float32) * eighth
        tab_c[0] = jnp.cos(phase) * scale
        tab_s[0] = jnp.sin(phase) * side * scale
        partners = []
        for b, q in enumerate(tile_qubits):
            partner, angle = jnp.int32(31), jnp.float32(0.0)
            for k in range(10):
                is_first, is_second = first[k] == q, second[k] == q
                partner = jnp.where(is_first, second[k], jnp.where(is_second, first[k], partner))
                angle = jnp.where(is_first | is_second, theta[k], angle)
            partners.append(partner)
            own = (linear[q] & 7).astype(jnp.float32) * eighth
            bit = ((n0 >> partner) & 1).astype(jnp.float32)
            zero = own + angle * bit
            fac_c[2 * b] = jnp.cos(zero)
            fac_s[2 * b] = jnp.sin(zero) * side
            one = zero * 0.0 + (own + angle)
            fac_c[2 * b + 1] = jnp.cos(one)
            fac_s[2 * b + 1] = jnp.sin(one) * side
        for b in range(9):
            count = 1 << b
            group = min(count, 8)

            def level(i, _, b=b, count=count, group=group):
                n_i = jnp.int32(0)
                for bit in range(3, b):
                    n_i = n_i | (((i >> (bit - 3)) & 1) << tile_qubits[bit])
                for u in range(group):
                    n_u = sum(1 << tile_qubits[bit] for bit in range(3) if (u >> bit) & 1)
                    sel = ((n_i | n_u) >> partners[b]) & 1
                    t = i * group + u
                    fc, fs = fac_c[2 * b + sel], fac_s[2 * b + sel]
                    tc, ts = tab_c[t], tab_s[t]
                    tab_c[t + count] = tc * fc - ts * fs
                    tab_s[t + count] = ts * fc + tc * fs
                return 0

            lax.fori_loop(0, count // group, level, 0)

    lin_mid = [choose(PHASE_OUT, picks[0, q]) + choose(PHASE_IN, picks[1, q]) for q in range(25)]
    const_mid = functools.reduce(lambda a, b: a + b, [choose(PHASE_ALL, picks[0, q]) for q in range(25)])
    phase_table(0, me << 11, 18, lin_mid, const_mid, 2.0**-12)

    row_i = lax.broadcasted_iota(jnp.int32, (256, 128), 0)
    col_i = lax.broadcasted_iota(jnp.int32, (256, 128), 1)
    lanes_mat[...] = parity_sign(row_i & col_i & 127).astype(jnp.bfloat16)
    row_j = lax.broadcasted_iota(jnp.int32, (256, 256), 0)
    col_j = lax.broadcasted_iota(jnp.int32, (256, 256), 1)
    same = ((row_j ^ col_j) & 4) == 0
    rows_mat[...] = jnp.where(same, parity_sign(row_j & col_j & 251), 0.0).astype(jnp.bfloat16)

    def mix_lanes(value):
        return jnp.dot(split(value), lanes_mat[...], preferred_element_type=jnp.float32)

    def mix_rows(value):
        wide = jnp.dot(rows_mat[...], split(value), preferred_element_type=jnp.float32)
        return wide[:, :128] + wide[:, 128:]

    def middle(j):
        source, target = slot_of(0, 4, j), slot_of(1, 0, j)

        def before(x, _):
            value = st[source, x].reshape(256, 128)
            work[x] = mix_rows(mix_lanes(value)).reshape(4, 4, 2, 8, 128)
            return 0

        def between(i, _):
            for u in range(2):
                y, z, c = i // 4, i % 4, u
                tiles = hadamard([work[x, y, z, c] for x in range(4)])
                for x in range(4):
                    t = j * 128 + x * 32 + i * 2 + u
                    tiles[x] = tiles[x] * tab_c[t] + swap(tiles[x]) * tab_s[t]
                tiles = hadamard(tiles)
                for x in range(4):
                    work[x, y, z, c] = tiles[x]
            return 0

        def after(x, _):
            value = work[x].reshape(256, 128)
            st[target, x] = mix_lanes(mix_rows(value)).reshape(4, 4, 2, 8, 128)
            return 0

        lax.fori_loop(0, 4, before, 0)
        lax.fori_loop(0, 16, between, 0)
        lax.fori_loop(0, 4, after, 0)

    travel(0)
    for j in (2, 0, 1, 3):
        arrived_step(0, j, 3, 0)
        middle(j)
        for h in (1, 0):
            send_step(1, j, 0, h)

    lin_end = [choose(PHASE_OUT, picks[1, q]) for q in range(25)]
    const_end = functools.reduce(lambda a, b: a + b, [choose(PHASE_ALL, picks[1, q]) for q in range(25)])
    phase_table(1, me << 18, 11, lin_end, const_end, 2.0**-13)
    sent(0, range(4))

    travel(1)
    for n, j in enumerate((2, 0, 1, 3)):
        arrived_step(1, j, 3, 0)
        walsh_rows(slot_of(1, 4, j), n)

    tile_of = lax.broadcasted_iota(jnp.int32, (128, 1024), 1) >> 3
    number = functools.reduce(
        lambda a, b: a | b, [((tile_of >> b) & 1) << ROW_BITS[b] for b in range(7)]
    )
    pick_rows = (number == lax.broadcasted_iota(jnp.int32, (128, 1024), 0)).astype(jnp.float32).astype(jnp.bfloat16)
    wide = jnp.dot(pick_rows, split(acc[...].reshape(1024, 128)), preferred_element_type=jnp.float32)
    by_row = wide[:, :128] + wide[:, 128:]
    row_mass = jnp.sum(by_row.T, axis=0, keepdims=True)
    own_a = pos["z"] * 2 + pos["c"]
    mass_a[own_a] = jnp.broadcast_to(row_mass, (8, 128))
    for z in range(4):
        for c in range(2):
            if z or c:
                pltpu.make_async_remote_copy(
                    mass_a.at[own_a],
                    mass_a.at[own_a],
                    mass_send.at[0],
                    mass_recv.at[0],
                    device_id=moved(pos, z=z, c=c),
                    device_id_type=MESH,
                ).start()

    def last_rows(i, _):
        xh, z, y = i // 16, (i // 4) % 4, i % 4
        for xl in range(2):
            for c in range(2):
                m = i * 4 + xl * 2 + c
                x = 2 * xh + xl
                r = ((x * 4 + y) * 4 + z) * 2 + c
                tiles = hadamard([st[slot_of(1, 4, j), x, y, z, c] for j in range(CHUNKS)])
                for j in range(CHUNKS):
                    tiles[j] = tiles[j] * tab_c[j * 128 + r] + swap(tiles[j]) * tab_s[j * 128 + r]
                for t in range(2):
                    p0, p1 = tiles[2 * t], tiles[2 * t + 1]
                    vout[0, m, pl.ds(8 * t, 8)] = jnp.where(top, p0, swap(p1))
                    vout[1, m, pl.ds(8 * t, 8)] = jnp.where(top, swap(p0), p1)
        return 0

    def store(b):
        rows = pl.ds(b * 16, 16)
        return pltpu.make_async_copy(vout.at[:, rows], out_hbm.at[:, rows], out_sem.at[b])

    for b in range(4):
        lax.fori_loop(b * 4, b * 4 + 4, last_rows, 0)
        store(b).start()

    seven = mass_a.at[pl.ds(0, 7)]
    pltpu.make_async_copy(seven, seven, mass_recv.at[0]).wait()
    own_b = pos["x"] * 4 + pos["y"]
    mass_b[own_b] = jnp.sum(mass_a[...], axis=0)
    for x in range(4):
        for y in range(4):
            if x or y:
                pltpu.make_async_remote_copy(
                    mass_b.at[own_b],
                    mass_b.at[own_b],
                    mass_send.at[1],
                    mass_recv.at[1],
                    device_id=moved(pos, x=x, y=y),
                    device_id_type=MESH,
                ).start()

    for b in range(4, 8):
        lax.fori_loop(b * 4, b * 4 + 4, last_rows, 0)
        store(b).start()

    sent(1, range(4))
    fifteen = mass_b.at[pl.ds(0, 15)]
    pltpu.make_async_copy(fifteen, fifteen, mass_recv.at[1]).wait()
    total = jnp.sum(mass_b[...], axis=0) * (2.0**-42)
    marginal_ref[...] = total[0:1]
    pltpu.make_async_copy(seven, seven, mass_send.at[0]).wait()
    pltpu.make_async_copy(fifteen, fifteen, mass_send.at[1]).wait()
    for b in range(8):
        store(b).wait()


def shards(amplitudes, gate_picks, pair_qubits, angles):
    rows = amplitudes.reshape(2, 128, 16, 128)
    f32 = jnp.float32
    final, marginal = pl.pallas_call(
        kernel,
        out_shape=(
            jax.ShapeDtypeStruct((2, 128, 16, 128), f32),
            jax.ShapeDtypeStruct((1, 128), f32),
        ),
        in_specs=[
            pl.BlockSpec(memory_space=pl.ANY),
            pl.BlockSpec(memory_space=pltpu.SMEM),
            pl.BlockSpec(memory_space=pltpu.SMEM),
            pl.BlockSpec(memory_space=pltpu.SMEM),
        ],
        out_specs=(
            pl.BlockSpec(memory_space=pl.ANY),
            pl.BlockSpec(memory_space=pltpu.VMEM),
        ),
        scratch_shapes=[
            pltpu.VMEM((40, 4, 4, 4, 2, 8, 128), f32),
            pltpu.VMEM((2, 128, 16, 128), f32),
            pltpu.VMEM((2, 128, 16, 128), f32),
            pltpu.VMEM((512, 8, 128), f32),
            pltpu.VMEM((512, 8, 128), f32),
            pltpu.VMEM((8, 8, 128), f32),
            pltpu.VMEM((8, 8, 128), f32),
            pltpu.VMEM((18, 8, 128), f32),
            pltpu.VMEM((18, 8, 128), f32),
            pltpu.VMEM((4, 4, 4, 2, 8, 128), f32),
            pltpu.VMEM((4, 4, 4, 2, 8, 128), f32),
            pltpu.VMEM((256, 128), jnp.bfloat16),
            pltpu.VMEM((256, 256), jnp.bfloat16),
            pltpu.VMEM((8, 8, 128), f32),
            pltpu.VMEM((16, 8, 128), f32),
            pltpu.SemaphoreType.DMA((8,)),
            pltpu.SemaphoreType.DMA((8,)),
            pltpu.SemaphoreType.DMA((2, 4, 4)),
            pltpu.SemaphoreType.DMA((2, 4, 4, 2)),
            pltpu.SemaphoreType.DMA((2, 4)),
            pltpu.SemaphoreType.DMA((2,)),
            pltpu.SemaphoreType.DMA((2,)),
        ],
        compiler_params=pltpu.CompilerParams(
            collective_id=0, has_side_effects=True, vmem_limit_bytes=52 << 20
        ),
        name="circuit",
    )(rows, gate_picks, pair_qubits, angles)
    return final.reshape(2, 1, 262144), marginal.reshape(128)


def solution(mesh):
    placed = (P(None, ("hi", "lo"), None), P(), P(), P())
    return jax.shard_map(
        shards,
        mesh=mesh,
        in_specs=placed,
        out_specs=(P(None, ("hi", "lo"), None), P()),
        check_vma=False,
    )
```

```python
import functools
import math

import jax
import jax.numpy as jnp
from jax import lax
from jax.experimental import pallas as pl
from jax.experimental.pallas import tpu as pltpu
from jax.sharding import PartitionSpec as P

MESH = pl.DeviceIdType.MESH

PHASE_IN = (-2, 4, 5)
PHASE_OUT = (-2, 0, -1)
PHASE_ALL = (1, 1, 0)

ROW_BITS = (0, 4, 5, 2, 3, 1, 6)
CHUNK_QUBITS = (9, 10)
CHUNKS = 4
SIZE = {"x": 4, "y": 4, "z": 4, "c": 2}
DIM = {"x": 0, "y": 1, "z": 2, "c": 3}

ORDER = ("xczy", "yxcz", "zyxc", "czyx")


def coordinates():
    hi, lo = lax.axis_index("hi"), lax.axis_index("lo")
    return {
        "x": (hi // 4) * 2 + (lo // 2) % 2,
        "y": lo // 4,
        "z": hi % 4,
        "c": lo % 2,
    }


def device_at(pos):
    return ((pos["x"] // 2) * 4 + pos["z"], pos["y"] * 4 + (pos["x"] % 2) * 2 + pos["c"])


def moved(pos, **flips):
    return device_at({a: jnp.bitwise_xor(pos[a], flips[a]) if flips.get(a, 0) else pos[a] for a in pos})


def hadamard(tiles):
    tiles = list(tiles)
    step = 1
    while step < len(tiles):
        for i in range(len(tiles)):
            if not i & step:
                a, b = tiles[i], tiles[i + step]
                tiles[i], tiles[i + step] = a + b, a - b
        step *= 2
    return tiles


def choose(table, pick):
    return jnp.where(pick == 0, table[0], jnp.where(pick == 1, table[1], table[2]))


def parity_sign(value):
    value = value ^ (value >> 4)
    value = value ^ (value >> 2)
    value = value ^ (value >> 1)
    return 1.0 - 2.0 * (value & 1).astype(jnp.float32)


def split(value):
    high = value.astype(jnp.bfloat16)
    low = (value - high.astype(jnp.float32)).astype(jnp.bfloat16)
    return jnp.concatenate([high, low], axis=1)


def part(ref, slot, at):
    index = [slot] + [at.get(a, slice(None)) for a in "xyzc"]
    return ref.at[tuple(index)]


def kernel(
    x_hbm,
    picks_hbm,
    pairs_hbm,
    angles_hbm,
    out_hbm,
    marginal_ref,
    st,
    picks,
    pairs,
    angles,
    vin,
    vout,
    tab_c,
    tab_s,
    in_c,
    in_s,
    fac_c,
    fac_s,
    work,
    acc,
    lanes_mat,
    rows_mat,
    pick_rows,
    mass_a,
    mass_b,
    in_sem,
    small_sem,
    out_sem,
    send_sem,
    recv_sem,
    last_sem,
    mass_send,
    mass_recv,
):
    pos = coordinates()
    me = lax.axis_index("hi") * 16 + lax.axis_index("lo")

    def load(b):
        rows = pl.ds(b * 16, 16)
        return pltpu.make_async_copy(x_hbm.at[:, rows], vin.at[:, rows], in_sem.at[b])

    small = [
        pltpu.make_async_copy(source, target, small_sem.at[n])
        for n, (source, target) in enumerate(((picks_hbm, picks), (pairs_hbm, pairs), (angles_hbm, angles)))
    ]
    small[0].start()
    for b in range(8):
        load(b).start()
    small[1].start()
    small[2].start()

    barrier = pltpu.get_barrier_semaphore()
    flips = [{"z": z, "c": c} for z in range(4) for c in range(2) if z or c]
    flips += [{"x": x, "y": y} for x in range(4) for y in range(4) if x or y]
    for flip in flips:
        pl.semaphore_signal(barrier, inc=1, device_id=moved(pos, **flip), device_id_type=MESH)

    lane = lax.broadcasted_iota(jnp.int32, (8, 128), 1)
    sub = lax.broadcasted_iota(jnp.int32, (8, 128), 0)
    top = sub < 4
    side = jnp.where(top, -1.0, 1.0)
    local_n = lane | ((sub & 3) << 7)
    eighth = math.pi / 4

    small[0].wait()
    lin_in = [choose(PHASE_IN, picks[0, q]) for q in range(25)]
    n_first = local_n | (me << 18)
    turn = jnp.zeros((8, 128), jnp.int32)
    for q in list(range(9)) + list(range(18, 25)):
        turn = turn + ((n_first >> q) & 1) * lin_in[q]
    for k in range(8):
        angle = ((turn + k) & 7).astype(jnp.float32) * eighth
        in_c[k] = jnp.cos(angle)
        in_s[k] = jnp.sin(angle) * side

    def swap(value):
        return pltpu.roll(value, 4, 0)

    def first_rows(i, _):
        xh, z, y = i // 16, (i // 4) % 4, i % 4
        k0 = xh * lin_in[17] + (z // 2) * lin_in[16] + (z % 2) * lin_in[15] + (y // 2) * lin_in[14] + (y % 2) * lin_in[13]
        for xl in range(2):
            for c in range(2):
                m = i * 4 + xl * 2 + c
                k1 = k0 + xl * lin_in[12] + c * lin_in[11]
                tiles = []
                for t in range(2):
                    re = vin[0, m, pl.ds(8 * t, 8)]
                    im = vin[1, m, pl.ds(8 * t, 8)]
                    rre, rim = swap(re), swap(im)
                    for e in range(2):
                        k = (k1 + t * lin_in[10] + e * lin_in[9]) & 7
                        if e == 0:
                            p, pr = jnp.where(top, re, rim), jnp.where(top, im, rre)
                        else:
                            p, pr = jnp.where(top, rre, im), jnp.where(top, rim, re)
                        tiles.append(p * in_c[k] + pr * in_s[k])
                tiles = hadamard(tiles)
                for j in range(CHUNKS):
                    st[j, 2 * xh + xl, y, z, c] = tiles[j]
        return 0

    for b in range(8):
        load(b).wait()
        lax.fori_loop(b * 4, b * 4 + 4, first_rows, 0)

    def walsh_rows(slot, mass=None):
        def pass_xy(i, _):
            z, c = i // 2, i % 2
            tiles = hadamard([st[slot, x, y, z, c] for x in range(4) for y in range(4)])
            for x in range(4):
                for y in range(4):
                    st[slot, x, y, z, c] = tiles[x * 4 + y]
            return 0

        def pass_zc(i, _):
            x, y = i // 4, i % 4
            tiles = hadamard([st[slot, x, y, z, c] for z in range(4) for c in range(2)])
            for z in range(4):
                for c in range(2):
                    tile = tiles[z * 2 + c]
                    st[slot, x, y, z, c] = tile
                    if mass == 0:
                        acc[x, y, z, c] = tile * tile
                    elif mass is not None:
                        acc[x, y, z, c] = acc[x, y, z, c] + tile * tile
            return 0

        lax.fori_loop(0, 8, pass_xy, 0)
        lax.fori_loop(0, 16, pass_zc, 0)

    def slot_of(e, i, j):
        return e * 20 + i * 4 + j

    def half(j, h):
        d = ORDER[j][3]
        width = SIZE[d] // 2
        return d, pl.ds(jnp.bitwise_xor(pos[d] // width, h) * width, width)

    def send_step(e, j, i, h):
        a = ORDER[j][i]
        if i < 3:
            d, piece = half(j, h)
            for flip in range(SIZE[a]):
                target = jnp.bitwise_xor(pos[a], flip) if flip else pos[a]
                src = part(st, slot_of(e, i, j), {a: target, d: piece})
                dst = part(st, slot_of(e, i + 1, j), {a: pos[a], d: piece})
                if flip:
                    pltpu.make_async_remote_copy(
                        src,
                        dst,
                        send_sem.at[e, j, i],
                        recv_sem.at[e, j, i, h],
                        device_id=moved(pos, **{a: flip}),
                        device_id_type=MESH,
                    ).start()
                else:
                    pltpu.make_async_copy(src, dst, recv_sem.at[e, j, i, h]).start()
        else:
            width = SIZE[a] // 2
            for flip in range(h * width, h * width + width):
                target = jnp.bitwise_xor(pos[a], flip) if flip else pos[a]
                src = part(st, slot_of(e, i, j), {a: target})
                dst = part(st, slot_of(e, i + 1, j), {a: pos[a]})
                if flip:
                    pltpu.make_async_remote_copy(
                        src,
                        dst,
                        send_sem.at[e, j, i],
                        last_sem.at[e, j],
                        device_id=moved(pos, **{a: flip}),
                        device_id_type=MESH,
                    ).start()
                else:
                    pltpu.make_async_copy(src, dst, last_sem.at[e, j]).start()

    def arrived_step(e, j, i, h):
        if i < 3:
            d, piece = half(j, h)
            ref = part(st, slot_of(e, i + 1, j), {d: piece})
            pltpu.make_async_copy(ref, ref, recv_sem.at[e, j, i, h]).wait()
        else:
            ref = st.at[slot_of(e, 4, j)]
            pltpu.make_async_copy(ref, ref, last_sem.at[e, j]).wait()

    def sent(e, steps):
        for j in range(CHUNKS):
            for i in steps:
                a = ORDER[j][i]
                ref = part(st, slot_of(e, i, j), {a: pl.ds(0, SIZE[a] * 3 // 4 if SIZE[a] == 4 else 1)})
                pltpu.make_async_copy(ref, ref, send_sem.at[e, j, i]).wait()

    def travel(e):
        for i in range(1, 4):
            for h in (1, 0):
                for j in range(CHUNKS):
                    arrived_step(e, j, i - 1, h)
                    send_step(e, j, i, h)

    pl.semaphore_wait(barrier, len(flips))
    for j in range(CHUNKS):
        walsh_rows(j)
        for h in (1, 0):
            send_step(0, j, 0, h)

    small[1].wait()
    small[2].wait()

    def phase_table(layer, n_base, row_base, linear, constant, scale):
        tile_qubits = [row_base + b for b in ROW_BITS] + list(CHUNK_QUBITS)
        other = [q for q in range(25) if q not in tile_qubits]
        first = [pairs[layer, 0, k] for k in range(10)]
        second = [pairs[layer, 1, k] for k in range(10)]
        theta = [angles[layer, k] for k in range(10)]
        n0 = local_n | n_base
        turns = jnp.full((8, 128), 0, jnp.int32) + constant
        for q in other:
            turns = turns + ((n0 >> q) & 1) * linear[q]
        phase = jnp.zeros((8, 128), jnp.float32)
        for k in range(10):
            both = (n0 >> first[k]) & (n0 >> second[k]) & 1
            phase = phase + theta[k] * both.astype(jnp.float32)
        phase = phase + (turns & 7).astype(jnp.float32) * eighth
        tab_c[0] = jnp.cos(phase) * scale
        tab_s[0] = jnp.sin(phase) * side * scale
        partners = []
        for b, q in enumerate(tile_qubits):
            partner, angle = jnp.int32(31), jnp.float32(0.0)
            for k in range(10):
                is_first, is_second = first[k] == q, second[k] == q
                partner = jnp.where(is_first, second[k], jnp.where(is_second, first[k], partner))
                angle = jnp.where(is_first | is_second, theta[k], angle)
            partners.append(partner)
            own = (linear[q] & 7).astype(jnp.float32) * eighth
            bit = ((n0 >> partner) & 1).astype(jnp.float32)
            zero = own + angle * bit
            fac_c[2 * b] = jnp.cos(zero)
            fac_s[2 * b] = jnp.sin(zero) * side
            one = zero * 0.0 + (own + angle)
            fac_c[2 * b + 1] = jnp.cos(one)
            fac_s[2 * b + 1] = jnp.sin(one) * side
        for b in range(9):
            count = 1 << b
            group = min(count, 8)

            def level(i, _, b=b, count=count, group=group):
                n_i = jnp.int32(0)
                for bit in range(3, b):
                    n_i = n_i | (((i >> (bit - 3)) & 1) << tile_qubits[bit])
                for u in range(group):
                    n_u = sum(1 << tile_qubits[bit] for bit in range(3) if (u >> bit) & 1)
                    sel = ((n_i | n_u) >> partners[b]) & 1
                    t = i * group + u
                    fc, fs = fac_c[2 * b + sel], fac_s[2 * b + sel]
                    tc, ts = tab_c[t], tab_s[t]
                    tab_c[t + count] = tc * fc - ts * fs
                    tab_s[t + count] = ts * fc + tc * fs
                return 0

            lax.fori_loop(0, count // group, level, 0)

    lin_mid = [choose(PHASE_OUT, picks[0, q]) + choose(PHASE_IN, picks[1, q]) for q in range(25)]
    const_mid = functools.reduce(lambda a, b: a + b, [choose(PHASE_ALL, picks[0, q]) for q in range(25)])
    phase_table(0, me << 11, 18, lin_mid, const_mid, 2.0**-12)

    row_i = lax.broadcasted_iota(jnp.int32, (256, 128), 0)
    col_i = lax.broadcasted_iota(jnp.int32, (256, 128), 1)
    lanes_mat[...] = parity_sign(row_i & col_i & 127).astype(jnp.bfloat16)
    row_j = lax.broadcasted_iota(jnp.int32, (256, 256), 0)
    col_j = lax.broadcasted_iota(jnp.int32, (256, 256), 1)
    same = ((row_j ^ col_j) & 4) == 0
    rows_mat[...] = jnp.where(same, parity_sign(row_j & col_j & 251), 0.0).astype(jnp.bfloat16)

    tile_of = lax.broadcasted_iota(jnp.int32, (128, 1024), 1) >> 3
    number = functools.reduce(
        lambda a, b: a | b, [((tile_of >> b) & 1) << ROW_BITS[b] for b in range(7)]
    )
    pick_rows[...] = (number == lax.broadcasted_iota(jnp.int32, (128, 1024), 0)).astype(jnp.float32).astype(jnp.bfloat16)

    def mix_lanes(value):
        return jnp.dot(split(value), lanes_mat[...], preferred_element_type=jnp.float32)

    def mix_rows(value):
        wide = jnp.dot(rows_mat[...], split(value), preferred_element_type=jnp.float32)
        return wide[:, :128] + wide[:, 128:]

    def middle(j):
        source, target = slot_of(0, 4, j), slot_of(1, 0, j)

        def before(x, _):
            value = st[source, x].reshape(256, 128)
            work[x] = mix_rows(mix_lanes(value)).reshape(4, 4, 2, 8, 128)
            return 0

        def between(i, _):
            for u in range(2):
                y, z, c = i // 4, i % 4, u
                tiles = hadamard([work[x, y, z, c] for x in range(4)])
                for x in range(4):
                    t = j * 128 + x * 32 + i * 2 + u
                    tiles[x] = tiles[x] * tab_c[t] + swap(tiles[x]) * tab_s[t]
                tiles = hadamard(tiles)
                for x in range(4):
                    work[x, y, z, c] = tiles[x]
            return 0

        def after(x, _):
            value = work[x].reshape(256, 128)
            st[target, x] = mix_lanes(mix_rows(value)).reshape(4, 4, 2, 8, 128)
            return 0

        for x in range(4):
            before(x, 0)
        lax.fori_loop(0, 16, between, 0)
        for x in range(4):
            after(x, 0)

    travel(0)
    for j in (2, 0, 1, 3):
        arrived_step(0, j, 3, 0)
        middle(j)
        for h in (1, 0):
            send_step(1, j, 0, h)

    lin_end = [choose(PHASE_OUT, picks[1, q]) for q in range(25)]
    const_end = functools.reduce(lambda a, b: a + b, [choose(PHASE_ALL, picks[1, q]) for q in range(25)])
    phase_table(1, me << 18, 11, lin_end, const_end, 2.0**-13)
    sent(0, range(4))

    travel(1)
    for n, j in enumerate((2, 0, 1, 3)):
        arrived_step(1, j, 3, 0)
        walsh_rows(slot_of(1, 4, j), n)

    wide = jnp.dot(pick_rows[...], split(acc[...].reshape(1024, 128)), preferred_element_type=jnp.float32)
    by_row = wide[:, :128] + wide[:, 128:]
    row_mass = jnp.sum(by_row.T, axis=0, keepdims=True)
    own_a = pos["z"] * 2 + pos["c"]
    mass_a[own_a] = jnp.broadcast_to(row_mass, (8, 128))
    for z in range(4):
        for c in range(2):
            if z or c:
                pltpu.make_async_remote_copy(
                    mass_a.at[own_a],
                    mass_a.at[own_a],
                    mass_send.at[0],
                    mass_recv.at[0],
                    device_id=moved(pos, z=z, c=c),
                    device_id_type=MESH,
                ).start()

    def last_rows(i, _):
        xh, z, y = i // 16, (i // 4) % 4, i % 4
        for xl in range(2):
            for c in range(2):
                m = i * 4 + xl * 2 + c
                x = 2 * xh + xl
                r = ((x * 4 + y) * 4 + z) * 2 + c
                tiles = hadamard([st[slot_of(1, 4, j), x, y, z, c] for j in range(CHUNKS)])
                for j in range(CHUNKS):
                    tiles[j] = tiles[j] * tab_c[j * 128 + r] + swap(tiles[j]) * tab_s[j * 128 + r]
                for t in range(2):
                    p0, p1 = tiles[2 * t], tiles[2 * t + 1]
                    vout[0, m, pl.ds(8 * t, 8)] = jnp.where(top, p0, swap(p1))
                    vout[1, m, pl.ds(8 * t, 8)] = jnp.where(top, swap(p0), p1)
        return 0

    def store(b):
        rows = pl.ds(b * 16, 16)
        return pltpu.make_async_copy(vout.at[:, rows], out_hbm.at[:, rows], out_sem.at[b])

    for b in range(4):
        lax.fori_loop(b * 4, b * 4 + 4, last_rows, 0)
        store(b).start()

    seven = mass_a.at[pl.ds(0, 7)]
    pltpu.make_async_copy(seven, seven, mass_recv.at[0]).wait()
    own_b = pos["x"] * 4 + pos["y"]
    mass_b[own_b] = jnp.sum(mass_a[...], axis=0)
    for x in range(4):
        for y in range(4):
            if x or y:
                pltpu.make_async_remote_copy(
                    mass_b.at[own_b],
                    mass_b.at[own_b],
                    mass_send.at[1],
                    mass_recv.at[1],
                    device_id=moved(pos, x=x, y=y),
                    device_id_type=MESH,
                ).start()

    for b in range(4, 8):
        lax.fori_loop(b * 4, b * 4 + 4, last_rows, 0)
        store(b).start()

    sent(1, range(4))
    fifteen = mass_b.at[pl.ds(0, 15)]
    pltpu.make_async_copy(fifteen, fifteen, mass_recv.at[1]).wait()
    total = jnp.sum(mass_b[...], axis=0) * (2.0**-42)
    marginal_ref[...] = total[0:1]
    pltpu.make_async_copy(seven, seven, mass_send.at[0]).wait()
    pltpu.make_async_copy(fifteen, fifteen, mass_send.at[1]).wait()
    for b in range(8):
        store(b).wait()


def place(state, mass, out_state, out_mass, held, in_sem, out_sem):
    def parts(n):
        return (n % 2, pl.ds(n // 2 * 16, 16))

    def fetch(n):
        return pltpu.make_async_copy(state.at[parts(n)], held.at[parts(n)], in_sem.at[n])

    def put(n):
        return pltpu.make_async_copy(held.at[parts(n)], out_state.at[parts(n)], out_sem.at[n])

    for n in range(16):
        fetch(n).start()
    out_mass[...] = mass[...]
    for n in range(16):
        fetch(n).wait()
        put(n).start()
    for n in range(16):
        put(n).wait()


def shards(amplitudes, gate_picks, pair_qubits, angles):
    rows = amplitudes.reshape(2, 128, 16, 128)
    f32 = jnp.float32
    state, mass = pl.pallas_call(
        kernel,
        out_shape=(
            jax.ShapeDtypeStruct((2, 128, 16, 128), f32),
            jax.ShapeDtypeStruct((1, 128), f32),
        ),
        in_specs=[
            pl.BlockSpec(memory_space=pltpu.HBM),
            pl.BlockSpec(memory_space=pltpu.HBM),
            pl.BlockSpec(memory_space=pltpu.HBM),
            pl.BlockSpec(memory_space=pltpu.HBM),
        ],
        out_specs=(
            pl.BlockSpec(memory_space=pl.ANY),
            pl.BlockSpec(memory_space=pltpu.VMEM),
        ),
        scratch_shapes=[
            pltpu.VMEM((40, 4, 4, 4, 2, 8, 128), f32),
            pltpu.SMEM((2, 25), jnp.int32),
            pltpu.SMEM((2, 2, 10), jnp.int32),
            pltpu.SMEM((2, 10), f32),
            pltpu.VMEM((2, 128, 16, 128), f32),
            pltpu.VMEM((2, 128, 16, 128), f32),
            pltpu.VMEM((512, 8, 128), f32),
            pltpu.VMEM((512, 8, 128), f32),
            pltpu.VMEM((8, 8, 128), f32),
            pltpu.VMEM((8, 8, 128), f32),
            pltpu.VMEM((18, 8, 128), f32),
            pltpu.VMEM((18, 8, 128), f32),
            pltpu.VMEM((4, 4, 4, 2, 8, 128), f32),
            pltpu.VMEM((4, 4, 4, 2, 8, 128), f32),
            pltpu.VMEM((256, 128), jnp.bfloat16),
            pltpu.VMEM((256, 256), jnp.bfloat16),
            pltpu.VMEM((128, 1024), jnp.bfloat16),
            pltpu.VMEM((8, 8, 128), f32),
            pltpu.VMEM((16, 8, 128), f32),
            pltpu.SemaphoreType.DMA((8,)),
            pltpu.SemaphoreType.DMA((3,)),
            pltpu.SemaphoreType.DMA((8,)),
            pltpu.SemaphoreType.DMA((2, 4, 4)),
            pltpu.SemaphoreType.DMA((2, 4, 4, 2)),
            pltpu.SemaphoreType.DMA((2, 4)),
            pltpu.SemaphoreType.DMA((2,)),
            pltpu.SemaphoreType.DMA((2,)),
        ],
        compiler_params=pltpu.CompilerParams(
            collective_id=0, has_side_effects=True, vmem_limit_bytes=63 << 20
        ),
        name="circuit",
    )(rows, gate_picks, pair_qubits.transpose(0, 2, 1), angles)
    final, marginal = pl.pallas_call(
        place,
        out_shape=(
            jax.ShapeDtypeStruct((2, 128, 16, 128), f32),
            jax.ShapeDtypeStruct((1, 128), f32),
        ),
        in_specs=[pl.BlockSpec(memory_space=pl.ANY), pl.BlockSpec(memory_space=pltpu.VMEM)],
        out_specs=(pl.BlockSpec(memory_space=pl.ANY), pl.BlockSpec(memory_space=pltpu.VMEM)),
        scratch_shapes=[
            pltpu.VMEM((2, 128, 16, 128), f32),
            pltpu.SemaphoreType.DMA((16,)),
            pltpu.SemaphoreType.DMA((16,)),
        ],
        compiler_params=pltpu.CompilerParams(vmem_limit_bytes=63 << 20),
        name="place",
    )(state, mass)
    return final.reshape(2, 1, 262144), marginal.reshape(128)


def solution(mesh):
    placed = (P(None, ("hi", "lo"), None), P(), P(), P())
    return jax.shard_map(
        shards,
        mesh=mesh,
        in_specs=placed,
        out_specs=(P(None, ("hi", "lo"), None), P()),
        check_vma=False,
    )
```

```python
import functools
import math

import jax
import jax.numpy as jnp
from jax import lax
from jax.experimental import pallas as pl
from jax.experimental.pallas import tpu as pltpu
from jax.sharding import PartitionSpec as P

MESH = pl.DeviceIdType.MESH

PHASE_IN = (-2, 4, 5)
PHASE_OUT = (-2, 0, -1)
PHASE_ALL = (1, 1, 0)

ROW_BITS = (0, 4, 5, 2, 3, 1, 6)
CHUNK_QUBITS = (9, 10)
CHUNKS = 4
SIZE = {"x": 4, "y": 4, "z": 4, "c": 2}
DIM = {"x": 0, "y": 1, "z": 2, "c": 3}

ORDER = ("xczy", "yxcz", "zyxc", "czyx")


def coordinates():
    hi, lo = lax.axis_index("hi"), lax.axis_index("lo")
    return {
        "x": (hi // 4) * 2 + (lo // 2) % 2,
        "y": lo // 4,
        "z": hi % 4,
        "c": lo % 2,
    }


def device_at(pos):
    return ((pos["x"] // 2) * 4 + pos["z"], pos["y"] * 4 + (pos["x"] % 2) * 2 + pos["c"])


def moved(pos, **flips):
    return device_at({a: jnp.bitwise_xor(pos[a], flips[a]) if flips.get(a, 0) else pos[a] for a in pos})


def hadamard(tiles):
    tiles = list(tiles)
    step = 1
    while step < len(tiles):
        for i in range(len(tiles)):
            if not i & step:
                a, b = tiles[i], tiles[i + step]
                tiles[i], tiles[i + step] = a + b, a - b
        step *= 2
    return tiles


def choose(table, pick):
    return jnp.where(pick == 0, table[0], jnp.where(pick == 1, table[1], table[2]))


def parity_sign(value):
    value = value ^ (value >> 4)
    value = value ^ (value >> 2)
    value = value ^ (value >> 1)
    return 1.0 - 2.0 * (value & 1).astype(jnp.float32)


def split(value):
    high = value.astype(jnp.bfloat16)
    low = (value - high.astype(jnp.float32)).astype(jnp.bfloat16)
    return jnp.concatenate([high, low], axis=1)


def part(ref, slot, at):
    index = [slot] + [at.get(a, slice(None)) for a in "xyzc"]
    return ref.at[tuple(index)]


def kernel(
    x_hbm,
    picks_hbm,
    pairs_hbm,
    angles_hbm,
    out_hbm,
    marginal_ref,
    st,
    picks,
    pairs,
    angles,
    vin,
    vout,
    tab_c,
    tab_s,
    in_c,
    in_s,
    fac_c,
    fac_s,
    work,
    acc,
    lanes_mat,
    rows_mat,
    pick_rows,
    mass_a,
    mass_b,
    in_sem,
    small_sem,
    out_sem,
    send_sem,
    recv_sem,
    last_sem,
    mass_send,
    mass_recv,
):
    pos = coordinates()
    me = lax.axis_index("hi") * 16 + lax.axis_index("lo")

    def load(b):
        rows = pl.ds(b * 16, 16)
        return pltpu.make_async_copy(x_hbm.at[:, rows], vin.at[:, rows], in_sem.at[b])

    small = [
        pltpu.make_async_copy(source, target, small_sem.at[n])
        for n, (source, target) in enumerate(((picks_hbm, picks), (pairs_hbm, pairs), (angles_hbm, angles)))
    ]
    small[0].start()
    for b in range(8):
        load(b).start()
    small[1].start()
    small[2].start()

    barrier = pltpu.get_barrier_semaphore()
    flips = [{"z": z, "c": c} for z in range(4) for c in range(2) if z or c]
    flips += [{"x": x, "y": y} for x in range(4) for y in range(4) if x or y]
    for flip in flips:
        pl.semaphore_signal(barrier, inc=1, device_id=moved(pos, **flip), device_id_type=MESH)

    lane = lax.broadcasted_iota(jnp.int32, (8, 128), 1)
    sub = lax.broadcasted_iota(jnp.int32, (8, 128), 0)
    top = sub < 4
    side = jnp.where(top, -1.0, 1.0)
    local_n = lane | ((sub & 3) << 7)
    eighth = math.pi / 4

    small[0].wait()
    lin_in = [choose(PHASE_IN, picks[0, q]) for q in range(25)]
    n_first = local_n | (me << 18)
    turn = jnp.zeros((8, 128), jnp.int32)
    for q in list(range(9)) + list(range(18, 25)):
        turn = turn + ((n_first >> q) & 1) * lin_in[q]
    for k in range(8):
        angle = ((turn + k) & 7).astype(jnp.float32) * eighth
        in_c[k] = jnp.cos(angle)
        in_s[k] = jnp.sin(angle) * side

    def swap(value):
        return pltpu.roll(value, 4, 0)

    def first_rows(i, _):
        xh, z, y = i // 16, (i // 4) % 4, i % 4
        k0 = xh * lin_in[17] + (z // 2) * lin_in[16] + (z % 2) * lin_in[15] + (y // 2) * lin_in[14] + (y % 2) * lin_in[13]
        for xl in range(2):
            for c in range(2):
                m = i * 4 + xl * 2 + c
                k1 = k0 + xl * lin_in[12] + c * lin_in[11]
                tiles = []
                for t in range(2):
                    re = vin[0, m, pl.ds(8 * t, 8)]
                    im = vin[1, m, pl.ds(8 * t, 8)]
                    rre, rim = swap(re), swap(im)
                    for e in range(2):
                        k = (k1 + t * lin_in[10] + e * lin_in[9]) & 7
                        if e == 0:
                            p, pr = jnp.where(top, re, rim), jnp.where(top, im, rre)
                        else:
                            p, pr = jnp.where(top, rre, im), jnp.where(top, rim, re)
                        tiles.append(p * in_c[k] + pr * in_s[k])
                tiles = hadamard(tiles)
                for j in range(CHUNKS):
                    st[j, 2 * xh + xl, y, z, c] = tiles[j]
        return 0

    for b in range(8):
        load(b).wait()
        lax.fori_loop(b * 4, b * 4 + 4, first_rows, 0, unroll=2)

    def walsh_rows(slot, mass=None):
        def pass_xy(i, _):
            z, c = i // 2, i % 2
            tiles = hadamard([st[slot, x, y, z, c] for x in range(4) for y in range(4)])
            for x in range(4):
                for y in range(4):
                    st[slot, x, y, z, c] = tiles[x * 4 + y]
            return 0

        def pass_zc(i, _):
            x, y = i // 4, i % 4
            tiles = hadamard([st[slot, x, y, z, c] for z in range(4) for c in range(2)])
            for z in range(4):
                for c in range(2):
                    tile = tiles[z * 2 + c]
                    st[slot, x, y, z, c] = tile
                    if mass == 0:
                        acc[x, y, z, c] = tile * tile
                    elif mass is not None:
                        acc[x, y, z, c] = acc[x, y, z, c] + tile * tile
            return 0

        lax.fori_loop(0, 8, pass_xy, 0, unroll=2)
        lax.fori_loop(0, 16, pass_zc, 0, unroll=4)

    def slot_of(e, i, j):
        return e * 20 + i * 4 + j

    def half(j, h):
        d = ORDER[j][3]
        width = SIZE[d] // 2
        return d, pl.ds(jnp.bitwise_xor(pos[d] // width, h) * width, width)

    def send_step(e, j, i, h):
        a = ORDER[j][i]
        if i < 3:
            d, piece = half(j, h)
            for flip in ((2, 1, 3, 0) if SIZE[a] == 4 else (1, 0)):
                target = jnp.bitwise_xor(pos[a], flip) if flip else pos[a]
                src = part(st, slot_of(e, i, j), {a: target, d: piece})
                dst = part(st, slot_of(e, i + 1, j), {a: pos[a], d: piece})
                if flip:
                    pltpu.make_async_remote_copy(
                        src,
                        dst,
                        send_sem.at[e, j, i],
                        recv_sem.at[e, j, i, h],
                        device_id=moved(pos, **{a: flip}),
                        device_id_type=MESH,
                    ).start()
                else:
                    dst[...] = src[...]
        else:
            width = SIZE[a] // 2
            for flip in range(h * width, h * width + width):
                target = jnp.bitwise_xor(pos[a], flip) if flip else pos[a]
                src = part(st, slot_of(e, i, j), {a: target})
                dst = part(st, slot_of(e, i + 1, j), {a: pos[a]})
                if flip:
                    pltpu.make_async_remote_copy(
                        src,
                        dst,
                        send_sem.at[e, j, i],
                        last_sem.at[e, j],
                        device_id=moved(pos, **{a: flip}),
                        device_id_type=MESH,
                    ).start()
                else:
                    dst[...] = src[...]

    def arrived_step(e, j, i, h):
        a = ORDER[j][i]
        rest = {a: pl.ds(0, SIZE[a] - 1)}
        if i < 3:
            d, piece = half(j, h)
            ref = part(st, slot_of(e, i + 1, j), {**rest, d: piece})
            pltpu.make_async_copy(ref, ref, recv_sem.at[e, j, i, h]).wait()
        else:
            ref = part(st, slot_of(e, 4, j), rest)
            pltpu.make_async_copy(ref, ref, last_sem.at[e, j]).wait()

    def sent(e, steps):
        for j in range(CHUNKS):
            for i in steps:
                a = ORDER[j][i]
                ref = part(st, slot_of(e, i, j), {a: pl.ds(0, SIZE[a] * 3 // 4 if SIZE[a] == 4 else 1)})
                pltpu.make_async_copy(ref, ref, send_sem.at[e, j, i]).wait()

    def travel(e):
        for i in range(1, 4):
            for h in (1, 0):
                for j in range(CHUNKS):
                    arrived_step(e, j, i - 1, h)
                    send_step(e, j, i, h)

    pl.semaphore_wait(barrier, len(flips))
    for j in range(CHUNKS):
        walsh_rows(j)
        for h in (1, 0):
            send_step(0, j, 0, h)

    small[1].wait()
    small[2].wait()

    def phase_table(layer, n_base, row_base, linear, constant, scale):
        tile_qubits = [row_base + b for b in ROW_BITS] + list(CHUNK_QUBITS)
        other = [q for q in range(25) if q not in tile_qubits]
        first = [pairs[layer, 0, k] for k in range(10)]
        second = [pairs[layer, 1, k] for k in range(10)]
        theta = [angles[layer, k] for k in range(10)]
        n0 = local_n | n_base
        turns = jnp.full((8, 128), 0, jnp.int32) + constant
        for q in other:
            turns = turns + ((n0 >> q) & 1) * linear[q]
        phase = jnp.zeros((8, 128), jnp.float32)
        for k in range(10):
            both = (n0 >> first[k]) & (n0 >> second[k]) & 1
            phase = phase + theta[k] * both.astype(jnp.float32)
        phase = phase + (turns & 7).astype(jnp.float32) * eighth
        tab_c[0] = jnp.cos(phase) * scale
        tab_s[0] = jnp.sin(phase) * side * scale
        partners = []
        for b, q in enumerate(tile_qubits):
            partner, angle = jnp.int32(31), jnp.float32(0.0)
            for k in range(10):
                is_first, is_second = first[k] == q, second[k] == q
                partner = jnp.where(is_first, second[k], jnp.where(is_second, first[k], partner))
                angle = jnp.where(is_first | is_second, theta[k], angle)
            partners.append(partner)
            own = (linear[q] & 7).astype(jnp.float32) * eighth
            bit = ((n0 >> partner) & 1).astype(jnp.float32)
            zero = own + angle * bit
            fac_c[2 * b] = jnp.cos(zero)
            fac_s[2 * b] = jnp.sin(zero) * side
            one = zero * 0.0 + (own + angle)
            fac_c[2 * b + 1] = jnp.cos(one)
            fac_s[2 * b + 1] = jnp.sin(one) * side
        for b in range(9):
            count = 1 << b
            group = min(count, 8)

            def level(i, _, b=b, count=count, group=group):
                n_i = jnp.int32(0)
                for bit in range(3, b):
                    n_i = n_i | (((i >> (bit - 3)) & 1) << tile_qubits[bit])
                for u in range(group):
                    n_u = sum(1 << tile_qubits[bit] for bit in range(3) if (u >> bit) & 1)
                    sel = ((n_i | n_u) >> partners[b]) & 1
                    t = i * group + u
                    fc, fs = fac_c[2 * b + sel], fac_s[2 * b + sel]
                    tc, ts = tab_c[t], tab_s[t]
                    tab_c[t + count] = tc * fc - ts * fs
                    tab_s[t + count] = ts * fc + tc * fs
                return 0

            lax.fori_loop(0, count // group, level, 0)

    lin_mid = [choose(PHASE_OUT, picks[0, q]) + choose(PHASE_IN, picks[1, q]) for q in range(25)]
    const_mid = functools.reduce(lambda a, b: a + b, [choose(PHASE_ALL, picks[0, q]) for q in range(25)])
    phase_table(0, me << 11, 18, lin_mid, const_mid, 2.0**-12)

    row_i = lax.broadcasted_iota(jnp.int32, (256, 128), 0)
    col_i = lax.broadcasted_iota(jnp.int32, (256, 128), 1)
    lanes_mat[...] = parity_sign(row_i & col_i & 127).astype(jnp.bfloat16)
    row_j = lax.broadcasted_iota(jnp.int32, (256, 256), 0)
    col_j = lax.broadcasted_iota(jnp.int32, (256, 256), 1)
    same = ((row_j ^ col_j) & 4) == 0
    rows_mat[...] = jnp.where(same, parity_sign(row_j & col_j & 251), 0.0).astype(jnp.bfloat16)

    tile_of = lax.broadcasted_iota(jnp.int32, (128, 1024), 1) >> 3
    number = functools.reduce(
        lambda a, b: a | b, [((tile_of >> b) & 1) << ROW_BITS[b] for b in range(7)]
    )
    pick_rows[...] = (number == lax.broadcasted_iota(jnp.int32, (128, 1024), 0)).astype(jnp.float32).astype(jnp.bfloat16)

    def mix_lanes(value):
        return jnp.dot(split(value), lanes_mat[...], preferred_element_type=jnp.float32)

    def mix_rows(value):
        wide = jnp.dot(rows_mat[...], split(value), preferred_element_type=jnp.float32)
        return wide[:, :128] + wide[:, 128:]

    def middle(j):
        source, target = slot_of(0, 4, j), slot_of(1, 0, j)

        def before(x, _):
            value = st[source, x].reshape(256, 128)
            work[x] = mix_rows(mix_lanes(value)).reshape(4, 4, 2, 8, 128)
            return 0

        def between(i, _):
            for u in range(2):
                y, z, c = i // 4, i % 4, u
                tiles = hadamard([work[x, y, z, c] for x in range(4)])
                for x in range(4):
                    t = j * 128 + x * 32 + i * 2 + u
                    tiles[x] = tiles[x] * tab_c[t] + swap(tiles[x]) * tab_s[t]
                tiles = hadamard(tiles)
                for x in range(4):
                    work[x, y, z, c] = tiles[x]
            return 0

        def after(x, _):
            value = work[x].reshape(256, 128)
            st[target, x] = mix_lanes(mix_rows(value)).reshape(4, 4, 2, 8, 128)
            return 0

        for x in range(4):
            before(x, 0)
        lax.fori_loop(0, 16, between, 0, unroll=4)
        for x in range(4):
            after(x, 0)

    travel(0)
    for j in (2, 0, 1, 3):
        arrived_step(0, j, 3, 0)
        middle(j)
        for h in (1, 0):
            send_step(1, j, 0, h)

    lin_end = [choose(PHASE_OUT, picks[1, q]) for q in range(25)]
    const_end = functools.reduce(lambda a, b: a + b, [choose(PHASE_ALL, picks[1, q]) for q in range(25)])
    phase_table(1, me << 18, 11, lin_end, const_end, 2.0**-13)
    sent(0, range(4))

    travel(1)
    for n, j in enumerate((2, 0, 1, 3)):
        arrived_step(1, j, 3, 0)
        walsh_rows(slot_of(1, 4, j), n)

    wide = jnp.dot(pick_rows[...], split(acc[...].reshape(1024, 128)), preferred_element_type=jnp.float32)
    by_row = wide[:, :128] + wide[:, 128:]
    row_mass = jnp.sum(by_row.T, axis=0, keepdims=True)
    own_a = pos["z"] * 2 + pos["c"]
    mass_a[own_a] = jnp.broadcast_to(row_mass, (8, 128))
    for z in range(4):
        for c in range(2):
            if z or c:
                pltpu.make_async_remote_copy(
                    mass_a.at[own_a],
                    mass_a.at[own_a],
                    mass_send.at[0],
                    mass_recv.at[0],
                    device_id=moved(pos, z=z, c=c),
                    device_id_type=MESH,
                ).start()

    def last_rows(i, _):
        xh, z, y = i // 16, (i // 4) % 4, i % 4
        for xl in range(2):
            for c in range(2):
                m = i * 4 + xl * 2 + c
                x = 2 * xh + xl
                r = ((x * 4 + y) * 4 + z) * 2 + c
                tiles = hadamard([st[slot_of(1, 4, j), x, y, z, c] for j in range(CHUNKS)])
                for j in range(CHUNKS):
                    tiles[j] = tiles[j] * tab_c[j * 128 + r] + swap(tiles[j]) * tab_s[j * 128 + r]
                for t in range(2):
                    p0, p1 = tiles[2 * t], tiles[2 * t + 1]
                    vout[0, m, pl.ds(8 * t, 8)] = jnp.where(top, p0, swap(p1))
                    vout[1, m, pl.ds(8 * t, 8)] = jnp.where(top, swap(p0), p1)
        return 0

    def store(b):
        rows = pl.ds(b * 16, 16)
        return pltpu.make_async_copy(vout.at[:, rows], out_hbm.at[:, rows], out_sem.at[b])

    for b in range(4):
        lax.fori_loop(b * 4, b * 4 + 4, last_rows, 0, unroll=2)
        store(b).start()

    seven = mass_a.at[pl.ds(0, 7)]
    pltpu.make_async_copy(seven, seven, mass_recv.at[0]).wait()
    own_b = pos["x"] * 4 + pos["y"]
    mass_b[own_b] = jnp.sum(mass_a[...], axis=0)
    for x in range(4):
        for y in range(4):
            if x or y:
                pltpu.make_async_remote_copy(
                    mass_b.at[own_b],
                    mass_b.at[own_b],
                    mass_send.at[1],
                    mass_recv.at[1],
                    device_id=moved(pos, x=x, y=y),
                    device_id_type=MESH,
                ).start()

    for b in range(4, 8):
        lax.fori_loop(b * 4, b * 4 + 4, last_rows, 0, unroll=2)
        store(b).start()

    sent(1, range(4))
    fifteen = mass_b.at[pl.ds(0, 15)]
    pltpu.make_async_copy(fifteen, fifteen, mass_recv.at[1]).wait()
    total = jnp.sum(mass_b[...], axis=0) * (2.0**-42)
    marginal_ref[...] = total[0:1]
    pltpu.make_async_copy(seven, seven, mass_send.at[0]).wait()
    pltpu.make_async_copy(fifteen, fifteen, mass_send.at[1]).wait()
    for b in range(8):
        store(b).wait()


def place(state, mass, out_state, out_mass, held, in_sem, out_sem):
    def parts(n):
        return (n % 2, pl.ds(n // 2 * 16, 16))

    def fetch(n):
        return pltpu.make_async_copy(state.at[parts(n)], held.at[parts(n)], in_sem.at[n])

    def put(n):
        return pltpu.make_async_copy(held.at[parts(n)], out_state.at[parts(n)], out_sem.at[n])

    for n in range(16):
        fetch(n).start()
    out_mass[...] = mass[...]
    for n in range(16):
        fetch(n).wait()
        put(n).start()
    for n in range(16):
        put(n).wait()


def shards(amplitudes, gate_picks, pair_qubits, angles):
    rows = amplitudes.reshape(2, 128, 16, 128)
    f32 = jnp.float32
    state, mass = pl.pallas_call(
        kernel,
        out_shape=(
            jax.ShapeDtypeStruct((2, 128, 16, 128), f32),
            jax.ShapeDtypeStruct((1, 128), f32),
        ),
        in_specs=[
            pl.BlockSpec(memory_space=pltpu.HBM),
            pl.BlockSpec(memory_space=pltpu.HBM),
            pl.BlockSpec(memory_space=pltpu.HBM),
            pl.BlockSpec(memory_space=pltpu.HBM),
        ],
        out_specs=(
            pl.BlockSpec(memory_space=pl.ANY),
            pl.BlockSpec(memory_space=pltpu.VMEM),
        ),
        scratch_shapes=[
            pltpu.VMEM((40, 4, 4, 4, 2, 8, 128), f32),
            pltpu.SMEM((2, 25), jnp.int32),
            pltpu.SMEM((2, 2, 10), jnp.int32),
            pltpu.SMEM((2, 10), f32),
            pltpu.VMEM((2, 128, 16, 128), f32),
            pltpu.VMEM((2, 128, 16, 128), f32),
            pltpu.VMEM((512, 8, 128), f32),
            pltpu.VMEM((512, 8, 128), f32),
            pltpu.VMEM((8, 8, 128), f32),
            pltpu.VMEM((8, 8, 128), f32),
            pltpu.VMEM((18, 8, 128), f32),
            pltpu.VMEM((18, 8, 128), f32),
            pltpu.VMEM((4, 4, 4, 2, 8, 128), f32),
            pltpu.VMEM((4, 4, 4, 2, 8, 128), f32),
            pltpu.VMEM((256, 128), jnp.bfloat16),
            pltpu.VMEM((256, 256), jnp.bfloat16),
            pltpu.VMEM((128, 1024), jnp.bfloat16),
            pltpu.VMEM((8, 8, 128), f32),
            pltpu.VMEM((16, 8, 128), f32),
            pltpu.SemaphoreType.DMA((8,)),
            pltpu.SemaphoreType.DMA((3,)),
            pltpu.SemaphoreType.DMA((8,)),
            pltpu.SemaphoreType.DMA((2, 4, 4)),
            pltpu.SemaphoreType.DMA((2, 4, 4, 2)),
            pltpu.SemaphoreType.DMA((2, 4)),
            pltpu.SemaphoreType.DMA((2,)),
            pltpu.SemaphoreType.DMA((2,)),
        ],
        compiler_params=pltpu.CompilerParams(
            collective_id=0, has_side_effects=True, vmem_limit_bytes=63 << 20
        ),
        name="circuit",
    )(rows, gate_picks, pair_qubits.transpose(0, 2, 1), angles)
    final, marginal = pl.pallas_call(
        place,
        out_shape=(
            jax.ShapeDtypeStruct((2, 128, 16, 128), f32),
            jax.ShapeDtypeStruct((1, 128), f32),
        ),
        in_specs=[pl.BlockSpec(memory_space=pl.ANY), pl.BlockSpec(memory_space=pltpu.VMEM)],
        out_specs=(pl.BlockSpec(memory_space=pl.ANY), pl.BlockSpec(memory_space=pltpu.VMEM)),
        scratch_shapes=[
            pltpu.VMEM((2, 128, 16, 128), f32),
            pltpu.SemaphoreType.DMA((16,)),
            pltpu.SemaphoreType.DMA((16,)),
        ],
        compiler_params=pltpu.CompilerParams(vmem_limit_bytes=63 << 20),
        name="place",
    )(state, mass)
    return final.reshape(2, 1, 262144), marginal.reshape(128)


def solution(mesh):
    placed = (P(None, ("hi", "lo"), None), P(), P(), P())
    return jax.shard_map(
        shards,
        mesh=mesh,
        in_specs=placed,
        out_specs=(P(None, ("hi", "lo"), None), P()),
        check_vma=False,
    )
```

```python
import functools
import math

import jax
import jax.numpy as jnp
from jax import lax
from jax.experimental import pallas as pl
from jax.experimental.pallas import tpu as pltpu
from jax.sharding import PartitionSpec as P

MESH = pl.DeviceIdType.MESH

PHASE_IN = (-2, 4, 5)
PHASE_OUT = (-2, 0, -1)
PHASE_ALL = (1, 1, 0)

ROW_BITS = (0, 4, 5, 2, 3, 1, 6)
CHUNK_QUBITS = (9, 10)
CHUNKS = 4
SIZE = {"x": 4, "y": 4, "z": 4, "c": 2}
DIM = {"x": 0, "y": 1, "z": 2, "c": 3}

ORDER = ("xczy", "yxcz", "zyxc", "czyx")


def coordinates():
    hi, lo = lax.axis_index("hi"), lax.axis_index("lo")
    return {
        "x": (hi // 4) * 2 + (lo // 2) % 2,
        "y": lo // 4,
        "z": hi % 4,
        "c": lo % 2,
    }


def device_at(pos):
    return ((pos["x"] // 2) * 4 + pos["z"], pos["y"] * 4 + (pos["x"] % 2) * 2 + pos["c"])


def moved(pos, **flips):
    return device_at({a: jnp.bitwise_xor(pos[a], flips[a]) if flips.get(a, 0) else pos[a] for a in pos})


def hadamard(tiles):
    tiles = list(tiles)
    step = 1
    while step < len(tiles):
        for i in range(len(tiles)):
            if not i & step:
                a, b = tiles[i], tiles[i + step]
                tiles[i], tiles[i + step] = a + b, a - b
        step *= 2
    return tiles


def choose(table, pick):
    return jnp.where(pick == 0, table[0], jnp.where(pick == 1, table[1], table[2]))


def parity_sign(value):
    value = value ^ (value >> 4)
    value = value ^ (value >> 2)
    value = value ^ (value >> 1)
    return 1.0 - 2.0 * (value & 1).astype(jnp.float32)


def split(value):
    high = value.astype(jnp.bfloat16)
    low = (value - high.astype(jnp.float32)).astype(jnp.bfloat16)
    return jnp.concatenate([high, low], axis=1)


def part(ref, slot, at):
    index = [slot] + [at.get(a, slice(None)) for a in "xyzc"]
    return ref.at[tuple(index)]


def kernel(
    x_hbm,
    picks_hbm,
    pairs_hbm,
    angles_hbm,
    out_hbm,
    marginal_ref,
    st,
    picks,
    pairs,
    angles,
    vin,
    vout,
    tab_c,
    tab_s,
    in_c,
    in_s,
    fac_c,
    fac_s,
    work,
    acc,
    lanes_mat,
    rows_mat,
    pick_rows,
    mass_a,
    mass_b,
    in_sem,
    small_sem,
    out_sem,
    send_sem,
    recv_sem,
    last_sem,
    mass_send,
    mass_recv,
):
    pos = coordinates()
    me = lax.axis_index("hi") * 16 + lax.axis_index("lo")

    def load(b):
        rows = pl.ds(b * 16, 16)
        return pltpu.make_async_copy(x_hbm.at[:, rows], vin.at[:, rows], in_sem.at[b])

    small = [
        pltpu.make_async_copy(source, target, small_sem.at[n])
        for n, (source, target) in enumerate(((picks_hbm, picks), (pairs_hbm, pairs), (angles_hbm, angles)))
    ]
    small[0].start()
    for b in range(8):
        load(b).start()
    small[1].start()
    small[2].start()

    barrier = pltpu.get_barrier_semaphore()
    flips = [{"z": z, "c": c} for z in range(4) for c in range(2) if z or c]
    flips += [{"x": x, "y": y} for x in range(4) for y in range(4) if x or y]
    for flip in flips:
        pl.semaphore_signal(barrier, inc=1, device_id=moved(pos, **flip), device_id_type=MESH)

    lane = lax.broadcasted_iota(jnp.int32, (8, 128), 1)
    sub = lax.broadcasted_iota(jnp.int32, (8, 128), 0)
    top = sub < 4
    side = jnp.where(top, -1.0, 1.0)
    local_n = lane | ((sub & 3) << 7)
    eighth = math.pi / 4

    small[0].wait()
    lin_in = [choose(PHASE_IN, picks[0, q]) for q in range(25)]
    n_first = local_n | (me << 18)
    turn = jnp.zeros((8, 128), jnp.int32)
    for q in list(range(9)) + list(range(18, 25)):
        turn = turn + ((n_first >> q) & 1) * lin_in[q]
    for k in range(8):
        angle = ((turn + k) & 7).astype(jnp.float32) * eighth
        in_c[k] = jnp.cos(angle)
        in_s[k] = jnp.sin(angle) * side

    def swap(value):
        return pltpu.roll(value, 4, 0)

    def first_rows(i, _):
        xh, z, y = i // 16, (i // 4) % 4, i % 4
        k0 = xh * lin_in[17] + (z // 2) * lin_in[16] + (z % 2) * lin_in[15] + (y // 2) * lin_in[14] + (y % 2) * lin_in[13]
        for xl in range(2):
            for c in range(2):
                m = i * 4 + xl * 2 + c
                k1 = k0 + xl * lin_in[12] + c * lin_in[11]
                tiles = []
                for t in range(2):
                    re = vin[0, m, pl.ds(8 * t, 8)]
                    im = vin[1, m, pl.ds(8 * t, 8)]
                    rre, rim = swap(re), swap(im)
                    for e in range(2):
                        k = (k1 + t * lin_in[10] + e * lin_in[9]) & 7
                        if e == 0:
                            p, pr = jnp.where(top, re, rim), jnp.where(top, im, rre)
                        else:
                            p, pr = jnp.where(top, rre, im), jnp.where(top, rim, re)
                        tiles.append(p * in_c[k] + pr * in_s[k])
                tiles = hadamard(tiles)
                for j in range(CHUNKS):
                    st[j, 2 * xh + xl, y, z, c] = tiles[j]
        return 0

    for b in range(8):
        load(b).wait()
        lax.fori_loop(b * 4, b * 4 + 4, first_rows, 0, unroll=2)

    def walsh_rows(slot, mass=None):
        def pass_xy(i, _):
            z, c = i // 2, i % 2
            tiles = hadamard([st[slot, x, y, z, c] for x in range(4) for y in range(4)])
            for x in range(4):
                for y in range(4):
                    st[slot, x, y, z, c] = tiles[x * 4 + y]
            return 0

        def pass_zc(i, _):
            x, y = i // 4, i % 4
            tiles = hadamard([st[slot, x, y, z, c] for z in range(4) for c in range(2)])
            for z in range(4):
                for c in range(2):
                    tile = tiles[z * 2 + c]
                    st[slot, x, y, z, c] = tile
                    if mass == 0:
                        acc[x, y, z, c] = tile * tile
                    elif mass is not None:
                        acc[x, y, z, c] = acc[x, y, z, c] + tile * tile
            return 0

        lax.fori_loop(0, 8, pass_xy, 0, unroll=2)
        lax.fori_loop(0, 16, pass_zc, 0, unroll=4)

    def slot_of(e, i, j):
        return e * 20 + i * 4 + j

    def half(j, h):
        d = ORDER[j][3]
        width = SIZE[d] // 2
        return d, pl.ds(jnp.bitwise_xor(pos[d] // width, h) * width, width)

    def send_step(e, j, i, h):
        a = ORDER[j][i]
        if i < 3:
            d, piece = half(j, h)
            for flip in ((2, 1, 3, 0) if SIZE[a] == 4 else (1, 0)):
                target = jnp.bitwise_xor(pos[a], flip) if flip else pos[a]
                src = part(st, slot_of(e, i, j), {a: target, d: piece})
                dst = part(st, slot_of(e, i + 1, j), {a: pos[a], d: piece})
                if flip:
                    pltpu.make_async_remote_copy(
                        src,
                        dst,
                        send_sem.at[e, j, i],
                        recv_sem.at[e, j, i, h],
                        device_id=moved(pos, **{a: flip}),
                        device_id_type=MESH,
                    ).start()
                else:
                    dst[...] = src[...]
        else:
            width = SIZE[a] // 2
            for flip in range(h * width, h * width + width):
                target = jnp.bitwise_xor(pos[a], flip) if flip else pos[a]
                src = part(st, slot_of(e, i, j), {a: target})
                dst = part(st, slot_of(e, i + 1, j), {a: pos[a]})
                if flip:
                    pltpu.make_async_remote_copy(
                        src,
                        dst,
                        send_sem.at[e, j, i],
                        last_sem.at[e, j],
                        device_id=moved(pos, **{a: flip}),
                        device_id_type=MESH,
                    ).start()
                else:
                    dst[...] = src[...]

    def arrived_step(e, j, i, h):
        a = ORDER[j][i]
        rest = {a: pl.ds(0, SIZE[a] - 1)}
        if i < 3:
            d, piece = half(j, h)
            ref = part(st, slot_of(e, i + 1, j), {**rest, d: piece})
            pltpu.make_async_copy(ref, ref, recv_sem.at[e, j, i, h]).wait()
        else:
            ref = part(st, slot_of(e, 4, j), rest)
            pltpu.make_async_copy(ref, ref, last_sem.at[e, j]).wait()

    def sent(e, steps):
        for j in range(CHUNKS):
            for i in steps:
                a = ORDER[j][i]
                ref = part(st, slot_of(e, i, j), {a: pl.ds(0, SIZE[a] * 3 // 4 if SIZE[a] == 4 else 1)})
                pltpu.make_async_copy(ref, ref, send_sem.at[e, j, i]).wait()

    def travel(e):
        for i in range(1, 4):
            for h in (1, 0):
                for j in range(CHUNKS):
                    arrived_step(e, j, i - 1, h)
                    send_step(e, j, i, h)

    pl.semaphore_wait(barrier, len(flips))
    for j in range(CHUNKS):
        walsh_rows(j)
        send_step(0, j, 0, 1)
    for j in range(CHUNKS):
        send_step(0, j, 0, 0)

    small[1].wait()
    small[2].wait()

    def phase_table(layer, n_base, row_base, linear, constant, scale):
        tile_qubits = [row_base + b for b in ROW_BITS] + list(CHUNK_QUBITS)
        other = [q for q in range(25) if q not in tile_qubits]
        first = [pairs[layer, 0, k] for k in range(10)]
        second = [pairs[layer, 1, k] for k in range(10)]
        theta = [angles[layer, k] for k in range(10)]
        n0 = local_n | n_base
        turns = jnp.full((8, 128), 0, jnp.int32) + constant
        for q in other:
            turns = turns + ((n0 >> q) & 1) * linear[q]
        phase = jnp.zeros((8, 128), jnp.float32)
        for k in range(10):
            both = (n0 >> first[k]) & (n0 >> second[k]) & 1
            phase = phase + theta[k] * both.astype(jnp.float32)
        phase = phase + (turns & 7).astype(jnp.float32) * eighth
        tab_c[0] = jnp.cos(phase) * scale
        tab_s[0] = jnp.sin(phase) * side * scale
        partners = []
        for b, q in enumerate(tile_qubits):
            partner, angle = jnp.int32(31), jnp.float32(0.0)
            for k in range(10):
                is_first, is_second = first[k] == q, second[k] == q
                partner = jnp.where(is_first, second[k], jnp.where(is_second, first[k], partner))
                angle = jnp.where(is_first | is_second, theta[k], angle)
            partners.append(partner)
            own = (linear[q] & 7).astype(jnp.float32) * eighth
            bit = ((n0 >> partner) & 1).astype(jnp.float32)
            zero = own + angle * bit
            fac_c[2 * b] = jnp.cos(zero)
            fac_s[2 * b] = jnp.sin(zero) * side
            one = zero * 0.0 + (own + angle)
            fac_c[2 * b + 1] = jnp.cos(one)
            fac_s[2 * b + 1] = jnp.sin(one) * side
        for b in range(9):
            count = 1 << b
            group = min(count, 8)

            def level(i, _, b=b, count=count, group=group):
                n_i = jnp.int32(0)
                for bit in range(3, b):
                    n_i = n_i | (((i >> (bit - 3)) & 1) << tile_qubits[bit])
                for u in range(group):
                    n_u = sum(1 << tile_qubits[bit] for bit in range(3) if (u >> bit) & 1)
                    sel = ((n_i | n_u) >> partners[b]) & 1
                    t = i * group + u
                    fc, fs = fac_c[2 * b + sel], fac_s[2 * b + sel]
                    tc, ts = tab_c[t], tab_s[t]
                    tab_c[t + count] = tc * fc - ts * fs
                    tab_s[t + count] = ts * fc + tc * fs
                return 0

            lax.fori_loop(0, count // group, level, 0)

    lin_mid = [choose(PHASE_OUT, picks[0, q]) + choose(PHASE_IN, picks[1, q]) for q in range(25)]
    const_mid = functools.reduce(lambda a, b: a + b, [choose(PHASE_ALL, picks[0, q]) for q in range(25)])
    phase_table(0, me << 11, 18, lin_mid, const_mid, 2.0**-12)

    row_i = lax.broadcasted_iota(jnp.int32, (256, 128), 0)
    col_i = lax.broadcasted_iota(jnp.int32, (256, 128), 1)
    lanes_mat[...] = parity_sign(row_i & col_i & 127).astype(jnp.bfloat16)
    row_j = lax.broadcasted_iota(jnp.int32, (256, 256), 0)
    col_j = lax.broadcasted_iota(jnp.int32, (256, 256), 1)
    same = ((row_j ^ col_j) & 4) == 0
    rows_mat[...] = jnp.where(same, parity_sign(row_j & col_j & 251), 0.0).astype(jnp.bfloat16)

    tile_of = lax.broadcasted_iota(jnp.int32, (128, 1024), 1) >> 3
    number = functools.reduce(
        lambda a, b: a | b, [((tile_of >> b) & 1) << ROW_BITS[b] for b in range(7)]
    )
    pick_rows[...] = (number == lax.broadcasted_iota(jnp.int32, (128, 1024), 0)).astype(jnp.float32).astype(jnp.bfloat16)

    def mix_lanes(value):
        return jnp.dot(split(value), lanes_mat[...], preferred_element_type=jnp.float32)

    def mix_rows(value):
        wide = jnp.dot(rows_mat[...], split(value), preferred_element_type=jnp.float32)
        return wide[:, :128] + wide[:, 128:]

    def middle(j):
        source, target = slot_of(0, 4, j), slot_of(1, 0, j)

        def before(x, _):
            value = st[source, x].reshape(256, 128)
            work[x] = mix_rows(mix_lanes(value)).reshape(4, 4, 2, 8, 128)
            return 0

        def between(i, _):
            for u in range(2):
                y, z, c = i // 4, i % 4, u
                tiles = hadamard([work[x, y, z, c] for x in range(4)])
                for x in range(4):
                    t = j * 128 + x * 32 + i * 2 + u
                    tiles[x] = tiles[x] * tab_c[t] + swap(tiles[x]) * tab_s[t]
                tiles = hadamard(tiles)
                for x in range(4):
                    work[x, y, z, c] = tiles[x]
            return 0

        def after(x, _):
            value = work[x].reshape(256, 128)
            st[target, x] = mix_lanes(mix_rows(value)).reshape(4, 4, 2, 8, 128)
            return 0

        for x in range(4):
            before(x, 0)
        lax.fori_loop(0, 16, between, 0, unroll=4)
        for x in range(4):
            after(x, 0)

    travel(0)
    for j in (2, 0, 1, 3):
        arrived_step(0, j, 3, 0)
        middle(j)
        for h in (1, 0):
            send_step(1, j, 0, h)

    lin_end = [choose(PHASE_OUT, picks[1, q]) for q in range(25)]
    const_end = functools.reduce(lambda a, b: a + b, [choose(PHASE_ALL, picks[1, q]) for q in range(25)])
    phase_table(1, me << 18, 11, lin_end, const_end, 2.0**-13)
    sent(0, range(4))

    travel(1)
    for n, j in enumerate((2, 0, 1, 3)):
        arrived_step(1, j, 3, 0)
        walsh_rows(slot_of(1, 4, j), n)

    wide = jnp.dot(pick_rows[...], split(acc[...].reshape(1024, 128)), preferred_element_type=jnp.float32)
    by_row = wide[:, :128] + wide[:, 128:]
    row_mass = jnp.sum(by_row.T, axis=0, keepdims=True)
    own_a = pos["z"] * 2 + pos["c"]
    mass_a[own_a] = jnp.broadcast_to(row_mass, (8, 128))
    for z in range(4):
        for c in range(2):
            if z or c:
                pltpu.make_async_remote_copy(
                    mass_a.at[own_a],
                    mass_a.at[own_a],
                    mass_send.at[0],
                    mass_recv.at[0],
                    device_id=moved(pos, z=z, c=c),
                    device_id_type=MESH,
                ).start()

    def last_rows(i, _):
        xh, z, y = i // 16, (i // 4) % 4, i % 4
        for xl in range(2):
            for c in range(2):
                m = i * 4 + xl * 2 + c
                x = 2 * xh + xl
                r = ((x * 4 + y) * 4 + z) * 2 + c
                tiles = hadamard([st[slot_of(1, 4, j), x, y, z, c] for j in range(CHUNKS)])
                for j in range(CHUNKS):
                    tiles[j] = tiles[j] * tab_c[j * 128 + r] + swap(tiles[j]) * tab_s[j * 128 + r]
                for t in range(2):
                    p0, p1 = tiles[2 * t], tiles[2 * t + 1]
                    vout[0, m, pl.ds(8 * t, 8)] = jnp.where(top, p0, swap(p1))
                    vout[1, m, pl.ds(8 * t, 8)] = jnp.where(top, swap(p0), p1)
        return 0

    def store(b):
        rows = pl.ds(b * 16, 16)
        return pltpu.make_async_copy(vout.at[:, rows], out_hbm.at[:, rows], out_sem.at[b])

    for b in range(4):
        lax.fori_loop(b * 4, b * 4 + 4, last_rows, 0, unroll=2)
        store(b).start()

    seven = mass_a.at[pl.ds(0, 7)]
    pltpu.make_async_copy(seven, seven, mass_recv.at[0]).wait()
    own_b = pos["x"] * 4 + pos["y"]
    mass_b[own_b] = jnp.sum(mass_a[...], axis=0)
    for x in range(4):
        for y in range(4):
            if x or y:
                pltpu.make_async_remote_copy(
                    mass_b.at[own_b],
                    mass_b.at[own_b],
                    mass_send.at[1],
                    mass_recv.at[1],
                    device_id=moved(pos, x=x, y=y),
                    device_id_type=MESH,
                ).start()

    for b in range(4, 8):
        lax.fori_loop(b * 4, b * 4 + 4, last_rows, 0, unroll=2)
        store(b).start()

    sent(1, range(4))
    fifteen = mass_b.at[pl.ds(0, 15)]
    pltpu.make_async_copy(fifteen, fifteen, mass_recv.at[1]).wait()
    total = jnp.sum(mass_b[...], axis=0) * (2.0**-42)
    marginal_ref[...] = total[0:1]
    pltpu.make_async_copy(seven, seven, mass_send.at[0]).wait()
    pltpu.make_async_copy(fifteen, fifteen, mass_send.at[1]).wait()
    for b in range(8):
        store(b).wait()


def place(state, mass, out_state, out_mass, held, in_sem, out_sem):
    def parts(n):
        return (n % 2, pl.ds(n // 2 * 16, 16))

    def fetch(n):
        return pltpu.make_async_copy(state.at[parts(n)], held.at[parts(n)], in_sem.at[n])

    def put(n):
        return pltpu.make_async_copy(held.at[parts(n)], out_state.at[parts(n)], out_sem.at[n])

    for n in range(16):
        fetch(n).start()
    out_mass[...] = mass[...]
    for n in range(16):
        fetch(n).wait()
        put(n).start()
    for n in range(16):
        put(n).wait()


def shards(amplitudes, gate_picks, pair_qubits, angles):
    rows = amplitudes.reshape(2, 128, 16, 128)
    f32 = jnp.float32
    state, mass = pl.pallas_call(
        kernel,
        out_shape=(
            jax.ShapeDtypeStruct((2, 128, 16, 128), f32),
            jax.ShapeDtypeStruct((1, 128), f32),
        ),
        in_specs=[
            pl.BlockSpec(memory_space=pltpu.HBM),
            pl.BlockSpec(memory_space=pltpu.HBM),
            pl.BlockSpec(memory_space=pltpu.HBM),
            pl.BlockSpec(memory_space=pltpu.HBM),
        ],
        out_specs=(
            pl.BlockSpec(memory_space=pl.ANY),
            pl.BlockSpec(memory_space=pltpu.VMEM),
        ),
        scratch_shapes=[
            pltpu.VMEM((40, 4, 4, 4, 2, 8, 128), f32),
            pltpu.SMEM((2, 25), jnp.int32),
            pltpu.SMEM((2, 2, 10), jnp.int32),
            pltpu.SMEM((2, 10), f32),
            pltpu.VMEM((2, 128, 16, 128), f32),
            pltpu.VMEM((2, 128, 16, 128), f32),
            pltpu.VMEM((512, 8, 128), f32),
            pltpu.VMEM((512, 8, 128), f32),
            pltpu.VMEM((8, 8, 128), f32),
            pltpu.VMEM((8, 8, 128), f32),
            pltpu.VMEM((18, 8, 128), f32),
            pltpu.VMEM((18, 8, 128), f32),
            pltpu.VMEM((4, 4, 4, 2, 8, 128), f32),
            pltpu.VMEM((4, 4, 4, 2, 8, 128), f32),
            pltpu.VMEM((256, 128), jnp.bfloat16),
            pltpu.VMEM((256, 256), jnp.bfloat16),
            pltpu.VMEM((128, 1024), jnp.bfloat16),
            pltpu.VMEM((8, 8, 128), f32),
            pltpu.VMEM((16, 8, 128), f32),
            pltpu.SemaphoreType.DMA((8,)),
            pltpu.SemaphoreType.DMA((3,)),
            pltpu.SemaphoreType.DMA((8,)),
            pltpu.SemaphoreType.DMA((2, 4, 4)),
            pltpu.SemaphoreType.DMA((2, 4, 4, 2)),
            pltpu.SemaphoreType.DMA((2, 4)),
            pltpu.SemaphoreType.DMA((2,)),
            pltpu.SemaphoreType.DMA((2,)),
        ],
        compiler_params=pltpu.CompilerParams(
            collective_id=0, has_side_effects=True, vmem_limit_bytes=63 << 20
        ),
        name="circuit",
    )(rows, gate_picks, pair_qubits.transpose(0, 2, 1), angles)
    final, marginal = pl.pallas_call(
        place,
        out_shape=(
            jax.ShapeDtypeStruct((2, 128, 16, 128), f32),
            jax.ShapeDtypeStruct((1, 128), f32),
        ),
        in_specs=[pl.BlockSpec(memory_space=pl.ANY), pl.BlockSpec(memory_space=pltpu.VMEM)],
        out_specs=(pl.BlockSpec(memory_space=pl.ANY), pl.BlockSpec(memory_space=pltpu.VMEM)),
        scratch_shapes=[
            pltpu.VMEM((2, 128, 16, 128), f32),
            pltpu.SemaphoreType.DMA((16,)),
            pltpu.SemaphoreType.DMA((16,)),
        ],
        compiler_params=pltpu.CompilerParams(vmem_limit_bytes=63 << 20),
        name="place",
    )(state, mass)
    return final.reshape(2, 1, 262144), marginal.reshape(128)


def solution(mesh):
    placed = (P(None, ("hi", "lo"), None), P(), P(), P())
    return jax.shard_map(
        shards,
        mesh=mesh,
        in_specs=placed,
        out_specs=(P(None, ("hi", "lo"), None), P()),
        check_vma=False,
    )
```

```python
import functools
import math

import jax
import jax.numpy as jnp
from jax import lax
from jax.experimental import pallas as pl
from jax.experimental.pallas import tpu as pltpu
from jax.sharding import PartitionSpec as P

MESH = pl.DeviceIdType.MESH

PHASE_IN = (-2, 4, 5)
PHASE_OUT = (-2, 0, -1)
PHASE_ALL = (1, 1, 0)

ROW_BITS = (0, 4, 5, 2, 3, 1, 6)
CHUNK_QUBITS = (9, 10)
CHUNKS = 4
SIZE = {"x": 4, "y": 4, "z": 4, "c": 2}
DIM = {"x": 0, "y": 1, "z": 2, "c": 3}

ORDER = ("xczy", "yxcz", "zyxc", "czyx")


def coordinates():
    hi, lo = lax.axis_index("hi"), lax.axis_index("lo")
    return {
        "x": (hi // 4) * 2 + (lo // 2) % 2,
        "y": lo // 4,
        "z": hi % 4,
        "c": lo % 2,
    }


def device_at(pos):
    return ((pos["x"] // 2) * 4 + pos["z"], pos["y"] * 4 + (pos["x"] % 2) * 2 + pos["c"])


def moved(pos, **flips):
    return device_at({a: jnp.bitwise_xor(pos[a], flips[a]) if flips.get(a, 0) else pos[a] for a in pos})


def hadamard(tiles):
    tiles = list(tiles)
    step = 1
    while step < len(tiles):
        for i in range(len(tiles)):
            if not i & step:
                a, b = tiles[i], tiles[i + step]
                tiles[i], tiles[i + step] = a + b, a - b
        step *= 2
    return tiles


def choose(table, pick):
    return jnp.where(pick == 0, table[0], jnp.where(pick == 1, table[1], table[2]))


def parity_sign(value):
    value = value ^ (value >> 4)
    value = value ^ (value >> 2)
    value = value ^ (value >> 1)
    return 1.0 - 2.0 * (value & 1).astype(jnp.float32)


def split(value):
    high = value.astype(jnp.bfloat16)
    low = (value - high.astype(jnp.float32)).astype(jnp.bfloat16)
    return jnp.concatenate([high, low], axis=1)


def part(ref, slot, at):
    index = [slot] + [at.get(a, slice(None)) for a in "xyzc"]
    return ref.at[tuple(index)]


def kernel(
    x_hbm,
    picks_hbm,
    pairs_hbm,
    angles_hbm,
    out_hbm,
    marginal_ref,
    st,
    picks,
    pairs,
    angles,
    vin,
    vout,
    tab_c,
    tab_s,
    in_c,
    in_s,
    fac_c,
    fac_s,
    work,
    acc,
    lanes_mat,
    rows_mat,
    pick_rows,
    mass_a,
    mass_b,
    in_sem,
    small_sem,
    out_sem,
    send_sem,
    recv_sem,
    last_sem,
    mass_send,
    mass_recv,
):
    pos = coordinates()
    me = lax.axis_index("hi") * 16 + lax.axis_index("lo")

    def load(b):
        rows = pl.ds(b * 16, 16)
        return pltpu.make_async_copy(x_hbm.at[:, rows], vin.at[:, rows], in_sem.at[b])

    small = [
        pltpu.make_async_copy(source, target, small_sem.at[n])
        for n, (source, target) in enumerate(((picks_hbm, picks), (pairs_hbm, pairs), (angles_hbm, angles)))
    ]
    small[0].start()
    for b in range(8):
        load(b).start()
    small[1].start()
    small[2].start()

    barrier = pltpu.get_barrier_semaphore()
    flips = [{"z": z, "c": c} for z in range(4) for c in range(2) if z or c]
    flips += [{"x": x, "y": y} for x in range(4) for y in range(4) if x or y]
    for flip in flips:
        pl.semaphore_signal(barrier, inc=1, device_id=moved(pos, **flip), device_id_type=MESH)

    lane = lax.broadcasted_iota(jnp.int32, (8, 128), 1)
    sub = lax.broadcasted_iota(jnp.int32, (8, 128), 0)
    top = sub < 4
    side = jnp.where(top, -1.0, 1.0)
    local_n = lane | ((sub & 3) << 7)
    eighth = math.pi / 4

    small[0].wait()
    lin_in = [choose(PHASE_IN, picks[0, q]) for q in range(25)]
    n_first = local_n | (me << 18)
    turn = jnp.zeros((8, 128), jnp.int32)
    for q in list(range(9)) + list(range(18, 25)):
        turn = turn + ((n_first >> q) & 1) * lin_in[q]
    for k in range(8):
        angle = ((turn + k) & 7).astype(jnp.float32) * eighth
        in_c[k] = jnp.cos(angle)
        in_s[k] = jnp.sin(angle) * side

    def swap(value):
        return pltpu.roll(value, 4, 0)

    def first_rows(i, _):
        xh, z, y = i // 16, (i // 4) % 4, i % 4
        k0 = xh * lin_in[17] + (z // 2) * lin_in[16] + (z % 2) * lin_in[15] + (y // 2) * lin_in[14] + (y % 2) * lin_in[13]
        rows = []
        for xl in range(2):
            for c in range(2):
                m = i * 4 + xl * 2 + c
                k1 = k0 + xl * lin_in[12] + c * lin_in[11]
                tiles = []
                for t in range(2):
                    re = vin[0, m, pl.ds(8 * t, 8)]
                    im = vin[1, m, pl.ds(8 * t, 8)]
                    rre, rim = swap(re), swap(im)
                    for e in range(2):
                        k = (k1 + t * lin_in[10] + e * lin_in[9]) & 7
                        if e == 0:
                            p, pr = jnp.where(top, re, rim), jnp.where(top, im, rre)
                        else:
                            p, pr = jnp.where(top, rre, im), jnp.where(top, rim, re)
                        tiles.append(p * in_c[k] + pr * in_s[k])
                rows.append(hadamard(tiles))
        for j in range(CHUNKS):
            tiles = hadamard([row[j] for row in rows])
            for n in range(4):
                st[j, 2 * xh + n // 2, y, z, n % 2] = tiles[n]
        return 0

    for b in range(8):
        load(b).wait()
        lax.fori_loop(b * 4, b * 4 + 4, first_rows, 0, unroll=2)

    def walsh_rows(slot, mass=None):
        def pass_xy(i, _):
            z, c = i // 2, i % 2
            tiles = hadamard([st[slot, x, y, z, c] for x in range(4) for y in range(4)])
            for x in range(4):
                for y in range(4):
                    st[slot, x, y, z, c] = tiles[x * 4 + y]
            return 0

        def pass_zc(i, _):
            x, y = i // 4, i % 4
            tiles = hadamard([st[slot, x, y, z, c] for z in range(4) for c in range(2)])
            for z in range(4):
                for c in range(2):
                    tile = tiles[z * 2 + c]
                    st[slot, x, y, z, c] = tile
                    if mass == 0:
                        acc[x, y, z, c] = tile * tile
                    elif mass is not None:
                        acc[x, y, z, c] = acc[x, y, z, c] + tile * tile
            return 0

        lax.fori_loop(0, 8, pass_xy, 0, unroll=2)
        lax.fori_loop(0, 16, pass_zc, 0, unroll=4)

    def walsh_first(slot):
        def rest(i, _):
            places = [(2 * xh + i // 2, y, z, i % 2) for xh in range(2) for y in range(4) for z in range(4)]
            tiles = hadamard([st[(slot,) + place] for place in places])
            for place, tile in zip(places, tiles):
                st[(slot,) + place] = tile
            return 0

        lax.fori_loop(0, 4, rest, 0)

    def slot_of(e, i, j):
        return e * 20 + i * 4 + j

    def half(j, h):
        d = ORDER[j][3]
        width = SIZE[d] // 2
        return d, pl.ds(jnp.bitwise_xor(pos[d] // width, h) * width, width)

    def send_step(e, j, i, h):
        a = ORDER[j][i]
        if i < 3:
            d, piece = half(j, h)
            for flip in ((2, 1, 3, 0) if SIZE[a] == 4 else (1, 0)):
                target = jnp.bitwise_xor(pos[a], flip) if flip else pos[a]
                src = part(st, slot_of(e, i, j), {a: target, d: piece})
                dst = part(st, slot_of(e, i + 1, j), {a: pos[a], d: piece})
                if flip:
                    pltpu.make_async_remote_copy(
                        src,
                        dst,
                        send_sem.at[e, j, i],
                        recv_sem.at[e, j, i, h],
                        device_id=moved(pos, **{a: flip}),
                        device_id_type=MESH,
                    ).start()
                else:
                    dst[...] = src[...]
        else:
            width = SIZE[a] // 2
            for flip in range(h * width, h * width + width):
                target = jnp.bitwise_xor(pos[a], flip) if flip else pos[a]
                src = part(st, slot_of(e, i, j), {a: target})
                dst = part(st, slot_of(e, i + 1, j), {a: pos[a]})
                if flip:
                    pltpu.make_async_remote_copy(
                        src,
                        dst,
                        send_sem.at[e, j, i],
                        last_sem.at[e, j],
                        device_id=moved(pos, **{a: flip}),
                        device_id_type=MESH,
                    ).start()
                else:
                    dst[...] = src[...]

    def arrived_step(e, j, i, h):
        a = ORDER[j][i]
        rest = {a: pl.ds(0, SIZE[a] - 1)}
        if i < 3:
            d, piece = half(j, h)
            ref = part(st, slot_of(e, i + 1, j), {**rest, d: piece})
            pltpu.make_async_copy(ref, ref, recv_sem.at[e, j, i, h]).wait()
        else:
            ref = part(st, slot_of(e, 4, j), rest)
            pltpu.make_async_copy(ref, ref, last_sem.at[e, j]).wait()

    def sent(e, steps):
        for j in range(CHUNKS):
            for i in steps:
                a = ORDER[j][i]
                ref = part(st, slot_of(e, i, j), {a: pl.ds(0, SIZE[a] * 3 // 4 if SIZE[a] == 4 else 1)})
                pltpu.make_async_copy(ref, ref, send_sem.at[e, j, i]).wait()

    def travel(e):
        for i in range(1, 4):
            for h in (1, 0):
                for j in range(CHUNKS):
                    arrived_step(e, j, i - 1, h)
                    send_step(e, j, i, h)

    pl.semaphore_wait(barrier, len(flips))
    for j in range(CHUNKS):
        walsh_first(j)
        send_step(0, j, 0, 1)
    for j in range(CHUNKS):
        send_step(0, j, 0, 0)

    small[1].wait()
    small[2].wait()

    def phase_table(layer, n_base, row_base, linear, constant, scale):
        tile_qubits = [row_base + b for b in ROW_BITS] + list(CHUNK_QUBITS)
        other = [q for q in range(25) if q not in tile_qubits]
        first = [pairs[layer, 0, k] for k in range(10)]
        second = [pairs[layer, 1, k] for k in range(10)]
        theta = [angles[layer, k] for k in range(10)]
        n0 = local_n | n_base
        turns = jnp.full((8, 128), 0, jnp.int32) + constant
        for q in other:
            turns = turns + ((n0 >> q) & 1) * linear[q]
        phase = jnp.zeros((8, 128), jnp.float32)
        for k in range(10):
            both = (n0 >> first[k]) & (n0 >> second[k]) & 1
            phase = phase + theta[k] * both.astype(jnp.float32)
        phase = phase + (turns & 7).astype(jnp.float32) * eighth
        tab_c[0] = jnp.cos(phase) * scale
        tab_s[0] = jnp.sin(phase) * side * scale
        partners = []
        for b, q in enumerate(tile_qubits):
            partner, angle = jnp.int32(31), jnp.float32(0.0)
            for k in range(10):
                is_first, is_second = first[k] == q, second[k] == q
                partner = jnp.where(is_first, second[k], jnp.where(is_second, first[k], partner))
                angle = jnp.where(is_first | is_second, theta[k], angle)
            partners.append(partner)
            own = (linear[q] & 7).astype(jnp.float32) * eighth
            bit = ((n0 >> partner) & 1).astype(jnp.float32)
            zero = own + angle * bit
            fac_c[2 * b] = jnp.cos(zero)
            fac_s[2 * b] = jnp.sin(zero) * side
            one = zero * 0.0 + (own + angle)
            fac_c[2 * b + 1] = jnp.cos(one)
            fac_s[2 * b + 1] = jnp.sin(one) * side
        for b in range(9):
            count = 1 << b
            group = min(count, 8)

            def level(i, _, b=b, count=count, group=group):
                n_i = jnp.int32(0)
                for bit in range(3, b):
                    n_i = n_i | (((i >> (bit - 3)) & 1) << tile_qubits[bit])
                for u in range(group):
                    n_u = sum(1 << tile_qubits[bit] for bit in range(3) if (u >> bit) & 1)
                    sel = ((n_i | n_u) >> partners[b]) & 1
                    t = i * group + u
                    fc, fs = fac_c[2 * b + sel], fac_s[2 * b + sel]
                    tc, ts = tab_c[t], tab_s[t]
                    tab_c[t + count] = tc * fc - ts * fs
                    tab_s[t + count] = ts * fc + tc * fs
                return 0

            lax.fori_loop(0, count // group, level, 0)

    lin_mid = [choose(PHASE_OUT, picks[0, q]) + choose(PHASE_IN, picks[1, q]) for q in range(25)]
    const_mid = functools.reduce(lambda a, b: a + b, [choose(PHASE_ALL, picks[0, q]) for q in range(25)])
    phase_table(0, me << 11, 18, lin_mid, const_mid, 2.0**-12)

    row_i = lax.broadcasted_iota(jnp.int32, (256, 128), 0)
    col_i = lax.broadcasted_iota(jnp.int32, (256, 128), 1)
    lanes_mat[...] = parity_sign(row_i & col_i & 127).astype(jnp.bfloat16)
    row_j = lax.broadcasted_iota(jnp.int32, (256, 256), 0)
    col_j = lax.broadcasted_iota(jnp.int32, (256, 256), 1)
    same = ((row_j ^ col_j) & 4) == 0
    rows_mat[...] = jnp.where(same, parity_sign(row_j & col_j & 251), 0.0).astype(jnp.bfloat16)

    tile_of = lax.broadcasted_iota(jnp.int32, (128, 1024), 1) >> 3
    number = functools.reduce(
        lambda a, b: a | b, [((tile_of >> b) & 1) << ROW_BITS[b] for b in range(7)]
    )
    pick_rows[...] = (number == lax.broadcasted_iota(jnp.int32, (128, 1024), 0)).astype(jnp.float32).astype(jnp.bfloat16)

    def mix_lanes(value):
        return jnp.dot(split(value), lanes_mat[...], preferred_element_type=jnp.float32)

    def mix_rows(value):
        wide = jnp.dot(rows_mat[...], split(value), preferred_element_type=jnp.float32)
        return wide[:, :128] + wide[:, 128:]

    def middle(j):
        source, target = slot_of(0, 4, j), slot_of(1, 0, j)

        def before(x, _):
            value = st[source, x].reshape(256, 128)
            work[x] = mix_rows(mix_lanes(value)).reshape(4, 4, 2, 8, 128)
            return 0

        def between(i, _):
            for u in range(2):
                y, z, c = i // 4, i % 4, u
                tiles = hadamard([work[x, y, z, c] for x in range(4)])
                for x in range(4):
                    t = j * 128 + x * 32 + i * 2 + u
                    tiles[x] = tiles[x] * tab_c[t] + swap(tiles[x]) * tab_s[t]
                tiles = hadamard(tiles)
                for x in range(4):
                    work[x, y, z, c] = tiles[x]
            return 0

        def after(x, _):
            value = work[x].reshape(256, 128)
            st[target, x] = mix_lanes(mix_rows(value)).reshape(4, 4, 2, 8, 128)
            return 0

        for x in range(4):
            before(x, 0)
        lax.fori_loop(0, 16, between, 0, unroll=4)
        for x in range(4):
            after(x, 0)

    travel(0)
    for j in (2, 0, 1, 3):
        arrived_step(0, j, 3, 0)
        middle(j)
        for h in (1, 0):
            send_step(1, j, 0, h)

    lin_end = [choose(PHASE_OUT, picks[1, q]) for q in range(25)]
    const_end = functools.reduce(lambda a, b: a + b, [choose(PHASE_ALL, picks[1, q]) for q in range(25)])
    phase_table(1, me << 18, 11, lin_end, const_end, 2.0**-13)
    sent(0, range(4))

    travel(1)
    for n, j in enumerate((2, 0, 1, 3)):
        arrived_step(1, j, 3, 0)
        walsh_rows(slot_of(1, 4, j), n)

    wide = jnp.dot(pick_rows[...], split(acc[...].reshape(1024, 128)), preferred_element_type=jnp.float32)
    by_row = wide[:, :128] + wide[:, 128:]
    row_mass = jnp.sum(by_row.T, axis=0, keepdims=True)
    own_a = pos["z"] * 2 + pos["c"]
    mass_a[own_a] = jnp.broadcast_to(row_mass, (8, 128))
    for z in range(4):
        for c in range(2):
            if z or c:
                pltpu.make_async_remote_copy(
                    mass_a.at[own_a],
                    mass_a.at[own_a],
                    mass_send.at[0],
                    mass_recv.at[0],
                    device_id=moved(pos, z=z, c=c),
                    device_id_type=MESH,
                ).start()

    def last_rows(i, _):
        xh, z, y = i // 16, (i // 4) % 4, i % 4
        for xl in range(2):
            for c in range(2):
                m = i * 4 + xl * 2 + c
                x = 2 * xh + xl
                r = ((x * 4 + y) * 4 + z) * 2 + c
                tiles = hadamard([st[slot_of(1, 4, j), x, y, z, c] for j in range(CHUNKS)])
                for j in range(CHUNKS):
                    tiles[j] = tiles[j] * tab_c[j * 128 + r] + swap(tiles[j]) * tab_s[j * 128 + r]
                for t in range(2):
                    p0, p1 = tiles[2 * t], tiles[2 * t + 1]
                    vout[0, m, pl.ds(8 * t, 8)] = jnp.where(top, p0, swap(p1))
                    vout[1, m, pl.ds(8 * t, 8)] = jnp.where(top, swap(p0), p1)
        return 0

    def store(b):
        rows = pl.ds(b * 16, 16)
        return pltpu.make_async_copy(vout.at[:, rows], out_hbm.at[:, rows], out_sem.at[b])

    for b in range(4):
        lax.fori_loop(b * 4, b * 4 + 4, last_rows, 0, unroll=2)
        store(b).start()

    seven = mass_a.at[pl.ds(0, 7)]
    pltpu.make_async_copy(seven, seven, mass_recv.at[0]).wait()
    own_b = pos["x"] * 4 + pos["y"]
    mass_b[own_b] = jnp.sum(mass_a[...], axis=0)
    for x in range(4):
        for y in range(4):
            if x or y:
                pltpu.make_async_remote_copy(
                    mass_b.at[own_b],
                    mass_b.at[own_b],
                    mass_send.at[1],
                    mass_recv.at[1],
                    device_id=moved(pos, x=x, y=y),
                    device_id_type=MESH,
                ).start()

    for b in range(4, 8):
        lax.fori_loop(b * 4, b * 4 + 4, last_rows, 0, unroll=2)
        store(b).start()

    sent(1, range(4))
    fifteen = mass_b.at[pl.ds(0, 15)]
    pltpu.make_async_copy(fifteen, fifteen, mass_recv.at[1]).wait()
    total = jnp.sum(mass_b[...], axis=0) * (2.0**-42)
    marginal_ref[...] = total[0:1]
    pltpu.make_async_copy(seven, seven, mass_send.at[0]).wait()
    pltpu.make_async_copy(fifteen, fifteen, mass_send.at[1]).wait()
    for b in range(8):
        store(b).wait()


def place(state, mass, out_state, out_mass, held, in_sem, out_sem):
    def parts(n):
        return (n % 2, pl.ds(n // 2 * 16, 16))

    def fetch(n):
        return pltpu.make_async_copy(state.at[parts(n)], held.at[parts(n)], in_sem.at[n])

    def put(n):
        return pltpu.make_async_copy(held.at[parts(n)], out_state.at[parts(n)], out_sem.at[n])

    for n in range(16):
        fetch(n).start()
    out_mass[...] = mass[...]
    for n in range(16):
        fetch(n).wait()
        put(n).start()
    for n in range(16):
        put(n).wait()


def shards(amplitudes, gate_picks, pair_qubits, angles):
    rows = amplitudes.reshape(2, 128, 16, 128)
    f32 = jnp.float32
    state, mass = pl.pallas_call(
        kernel,
        out_shape=(
            jax.ShapeDtypeStruct((2, 128, 16, 128), f32),
            jax.ShapeDtypeStruct((1, 128), f32),
        ),
        in_specs=[
            pl.BlockSpec(memory_space=pltpu.HBM),
            pl.BlockSpec(memory_space=pltpu.HBM),
            pl.BlockSpec(memory_space=pltpu.HBM),
            pl.BlockSpec(memory_space=pltpu.HBM),
        ],
        out_specs=(
            pl.BlockSpec(memory_space=pl.ANY),
            pl.BlockSpec(memory_space=pltpu.VMEM),
        ),
        scratch_shapes=[
            pltpu.VMEM((40, 4, 4, 4, 2, 8, 128), f32),
            pltpu.SMEM((2, 25), jnp.int32),
            pltpu.SMEM((2, 2, 10), jnp.int32),
            pltpu.SMEM((2, 10), f32),
            pltpu.VMEM((2, 128, 16, 128), f32),
            pltpu.VMEM((2, 128, 16, 128), f32),
            pltpu.VMEM((512, 8, 128), f32),
            pltpu.VMEM((512, 8, 128), f32),
            pltpu.VMEM((8, 8, 128), f32),
            pltpu.VMEM((8, 8, 128), f32),
            pltpu.VMEM((18, 8, 128), f32),
            pltpu.VMEM((18, 8, 128), f32),
            pltpu.VMEM((4, 4, 4, 2, 8, 128), f32),
            pltpu.VMEM((4, 4, 4, 2, 8, 128), f32),
            pltpu.VMEM((256, 128), jnp.bfloat16),
            pltpu.VMEM((256, 256), jnp.bfloat16),
            pltpu.VMEM((128, 1024), jnp.bfloat16),
            pltpu.VMEM((8, 8, 128), f32),
            pltpu.VMEM((16, 8, 128), f32),
            pltpu.SemaphoreType.DMA((8,)),
            pltpu.SemaphoreType.DMA((3,)),
            pltpu.SemaphoreType.DMA((8,)),
            pltpu.SemaphoreType.DMA((2, 4, 4)),
            pltpu.SemaphoreType.DMA((2, 4, 4, 2)),
            pltpu.SemaphoreType.DMA((2, 4)),
            pltpu.SemaphoreType.DMA((2,)),
            pltpu.SemaphoreType.DMA((2,)),
        ],
        compiler_params=pltpu.CompilerParams(
            collective_id=0, has_side_effects=True, vmem_limit_bytes=63 << 20
        ),
        name="circuit",
    )(rows, gate_picks, pair_qubits.transpose(0, 2, 1), angles)
    final, marginal = pl.pallas_call(
        place,
        out_shape=(
            jax.ShapeDtypeStruct((2, 128, 16, 128), f32),
            jax.ShapeDtypeStruct((1, 128), f32),
        ),
        in_specs=[pl.BlockSpec(memory_space=pl.ANY), pl.BlockSpec(memory_space=pltpu.VMEM)],
        out_specs=(pl.BlockSpec(memory_space=pl.ANY), pl.BlockSpec(memory_space=pltpu.VMEM)),
        scratch_shapes=[
            pltpu.VMEM((2, 128, 16, 128), f32),
            pltpu.SemaphoreType.DMA((16,)),
            pltpu.SemaphoreType.DMA((16,)),
        ],
        compiler_params=pltpu.CompilerParams(vmem_limit_bytes=63 << 20),
        name="place",
    )(state, mass)
    return final.reshape(2, 1, 262144), marginal.reshape(128)


def solution(mesh):
    placed = (P(None, ("hi", "lo"), None), P(), P(), P())
    return jax.shard_map(
        shards,
        mesh=mesh,
        in_specs=placed,
        out_specs=(P(None, ("hi", "lo"), None), P()),
        check_vma=False,
    )
```
